1024 devices in a mesh: clus: 64 (over y, x, core), sub: 16 (over z).
Axes of the slice: x: 4, y: 8, z: 16, core: 2. Of those that a mesh axis runs over, the one named last changes fastest.
Arguments:
- schur: bfloat16 [64, 16, 512, 512], P('clus', 'sub'), as said below
- load: float32 [64, 16, 4, 16, 128], P('clus', 'sub')
- rigid: float32 [64, 16, 4, 6, 128], P('clus', 'sub')
- lengths: int32 [64, 16, 4], P('clus', 'sub'), may hold values from 0 to 128, as said below
- partner: int32 [64, 16, 4, 128], P('clus', 'sub'), may hold values from 0 to 127, as said below
- coarse_inverse: float32 [384, 384], replicated, as said below
Outputs:
- multipliers: float32 [64, 16, 4, 16, 128], P('clus', 'sub')
- residual: float32 [64, 16, 4, 16, 128], P('clus', 'sub')
The draws below stay inside these ranges and needn't reach their ends.
Inputs may be any that keep to these rules, and one draw needn't show every extreme that they name: `schur`: each subdomain's matrix is symmetric. `coarse_inverse`: symmetric. `lengths`: both sides of a neighbour pair hold the same length; 0 exactly where no neighbour exists; some pair has 128. On used rows, partner maps the used rows of a pair one to one onto the neighbour's used rows of the opposite direction, and the neighbour's partner maps them back; unused rows hold their own index.
All inputs are finite; a program needn't handle non-finite values.
Results may differ from the reference program's by a relative error of at most 0.0039.
Values sent between devices are 32-bit elements; how exact they have to be, the bound alone decides.
A program may use at most 32 MiB of HBM per device.

```python
import math
import jax
import jax.numpy as jnp
from jax import lax

PAIR = 128
CASES = 16
MODES = 6
ITERS = 2
NCL = 64
NSUB = 16
COARSE = 384
N_CLUS = 64
N_SUB = 16


def symmetric_block(key, count, order, low, high):
    key_off, key_diag = jax.random.split(key, 2)
    bound = 0.52 / math.sqrt(order)
    raw_part = jax.random.uniform(key_off, (count, order, order), jnp.float32, -bound, bound)
    off_part = (raw_part + jnp.swapaxes(raw_part, 1, 2)) * (1.0 / math.sqrt(2.0))
    eye_mat = jnp.eye(order, dtype=jnp.float32)
    diag_part = jax.random.uniform(key_diag, (count, order), jnp.float32, low, high)
    matrix = off_part * (1.0 - eye_mat) + eye_mat * diag_part[:, :, None]
    return matrix


def draw_schur(key, part):
    cluster_keys = jax.random.split(jax.random.fold_in(key, 101), NCL)

    def one_cluster(cluster_key):
        return symmetric_block(cluster_key, NSUB, 4 * PAIR, 1.0, 2.0).astype(jnp.bfloat16)
    return lax.map(one_cluster, cluster_keys)


def draw_coarse_inverse(key, part):
    return symmetric_block(jax.random.fold_in(key, 202), 1, COARSE, 0.8, 1.6)[0]


def rigid_modes(key):
    base_key = jax.random.fold_in(key, 303)
    shape = (NCL, NSUB, 4, MODES, PAIR)
    scale = 1.0 / math.sqrt(NSUB * 4 * PAIR)
    return jax.random.normal(base_key, shape, jnp.float32) * scale


def draw_rigid(key, part):
    return rigid_modes(key)


def draw_load(key, part):
    modes_part = rigid_modes(key)
    key_noise, key_mix = jax.random.split(jax.random.fold_in(key, 404))
    shape = (NCL, NSUB, 4, CASES, PAIR)
    cluster_rise = 0.5 + jnp.arange(NCL, dtype=jnp.float32) / max(NCL - 1, 1)
    noise = jax.random.normal(key_noise, shape, jnp.float32)
    mixing = jax.random.normal(key_mix, (NCL, MODES, CASES), jnp.float32) * (1.0 / math.sqrt(MODES))
    aligned = jnp.einsum('csdmp,cmj->csdjp', modes_part, mixing) * math.sqrt(NSUB * 4 * PAIR)
    return noise * cluster_rise[:, None, None, None, None] + aligned


def edge_tables(key):
    base_key = jax.random.fold_in(key, 55)
    key_len_sub, key_len_clus, key_score_sub, key_score_clus = jax.random.split(base_key, 4)
    len_sub = jax.random.randint(key_len_sub, (NCL, NSUB), PAIR // 4, PAIR + 1).astype(jnp.int32)
    len_sub = len_sub.at[0, 0].set(PAIR)
    len_clus = jax.random.randint(key_len_clus, (NCL, NSUB), PAIR // 4, PAIR + 1).astype(jnp.int32)
    row_ids = jnp.arange(PAIR, dtype=jnp.int32)

    def matchings(score_key, edge_len):
        score = jax.random.randint(score_key, edge_len.shape + (PAIR,), 0, 65536).astype(jnp.int32) * PAIR + row_ids
        score = jnp.where(row_ids < edge_len[..., None], score, 1073741824 + row_ids)
        forward = jnp.argsort(score, axis=-1).astype(jnp.int32)
        backward = jnp.argsort(forward, axis=-1).astype(jnp.int32)
        return (forward, backward)
    fwd_sub, back_sub = matchings(key_score_sub, len_sub)
    fwd_clus, back_clus = matchings(key_score_clus, len_clus)
    zero_sub = jnp.zeros((NCL, 1), jnp.int32)
    zero_clus = jnp.zeros((1, NSUB), jnp.int32)
    len_lo_sub = jnp.concatenate([zero_sub, len_sub[:, :-1]], axis=1)
    len_hi_sub = jnp.concatenate([len_sub[:, :-1], zero_sub], axis=1)
    len_lo_clus = jnp.concatenate([zero_clus, len_clus[:-1]], axis=0)
    len_hi_clus = jnp.concatenate([len_clus[:-1], zero_clus], axis=0)
    all_lengths = jnp.stack([len_lo_sub, len_hi_sub, len_lo_clus, len_hi_clus], axis=2)
    ident_sub = jnp.broadcast_to(row_ids, (NCL, 1, PAIR))
    ident_clus = jnp.broadcast_to(row_ids, (1, NSUB, PAIR))
    part_lo_sub = jnp.concatenate([ident_sub, back_sub[:, :-1]], axis=1)
    part_hi_sub = jnp.concatenate([fwd_sub[:, :-1], ident_sub], axis=1)
    part_lo_clus = jnp.concatenate([ident_clus, back_clus[:-1]], axis=0)
    part_hi_clus = jnp.concatenate([fwd_clus[:-1], ident_clus], axis=0)
    all_partners = jnp.stack([part_lo_sub, part_hi_sub, part_lo_clus, part_hi_clus], axis=2)
    return (all_lengths, all_partners)


def draw_lengths(key, part):
    return edge_tables(key)[0]


def draw_partner(key, part):
    return edge_tables(key)[1]


def setup_inputs(seed: int = 0) -> dict:
    streams_of = jax.random.split(jax.random.key(seed), 7)
    schur = draw_schur(jax.random.fold_in(streams_of[6], 71), 0)
    load = draw_load(jax.random.fold_in(streams_of[6], 71), 0)
    rigid = draw_rigid(jax.random.fold_in(streams_of[6], 71), 0)
    lengths = draw_lengths(jax.random.fold_in(streams_of[6], 71), 0)
    partner = draw_partner(jax.random.fold_in(streams_of[6], 71), 0)
    coarse_inverse = draw_coarse_inverse(jax.random.fold_in(streams_of[6], 71), 0)
    return dict(schur=schur, load=load, rigid=rigid, lengths=lengths, partner=partner, coarse_inverse=coarse_inverse)


FULL_PRECISION = lax.Precision.HIGHEST


def sign_table():
    return jnp.array([-1.0, 1.0, -1.0, 1.0], jnp.float32)


def far_side(values, partner):
    zero_sub = jnp.zeros_like(values[:, :1, 0])
    zero_clus = jnp.zeros_like(values[:1, :, 0])
    lower_sub = jnp.concatenate([zero_sub, values[:, :-1, 1]], axis=1)
    upper_sub = jnp.concatenate([values[:, 1:, 0], zero_sub], axis=1)
    lower_clus = jnp.concatenate([zero_clus, values[:-1, :, 3]], axis=0)
    upper_clus = jnp.concatenate([values[1:, :, 2], zero_clus], axis=0)
    arrived = jnp.stack([lower_sub, upper_sub, lower_clus, upper_clus], axis=2)
    gather_index = jnp.broadcast_to(partner[:, :, :, None, :], arrived.shape)
    return jnp.take_along_axis(arrived, gather_index, axis=4)


def reference(schur, load, rigid, lengths, partner, coarse_inverse):
    slot_index = lax.broadcasted_iota(jnp.int32, (N_CLUS, N_SUB, 4, PAIR), 3)
    live_rows = (slot_index < lengths[:, :, :, None]).astype(jnp.float32)
    sign_live = (sign_table()[None, None, :, None] * live_rows)[:, :, :, None, :]

    def jump_rows(values):
        return sign_live * (values - far_side(values, partner))

    diag_own = jnp.diagonal(schur, axis1=2, axis2=3).astype(jnp.float32).reshape(N_CLUS, N_SUB, 4, 1, PAIR)
    weight = live_rows[:, :, :, None, :] / (diag_own + far_side(diag_own, partner))
    dual_rhs = jump_rows(load)
    signed_rigid = rigid * sign_live

    def project(vector):
        coarse_sums = jnp.einsum("csdmp,csdjp->cmj", signed_rigid, vector, precision=FULL_PRECISION)
        coeffs = jnp.dot(coarse_inverse, coarse_sums.reshape(N_CLUS * MODES, CASES), precision=FULL_PRECISION)
        coeffs = coeffs.reshape(N_CLUS, MODES, CASES)
        expanded = jnp.einsum("csdmp,cmj->csdjp", rigid, coeffs, precision=FULL_PRECISION)
        return vector - jump_rows(expanded)

    def inner_dot(left_vec, right_vec):
        return 0.5 * jnp.sum(left_vec * right_vec, axis=(0, 1, 2, 4))

    def cluster_apply(pair_args):
        matrices, vectors = pair_args
        flattened = vectors.astype(jnp.float32).transpose(0, 2, 1, 3).reshape(N_SUB, CASES, 4 * PAIR)
        image_rows = jnp.einsum("sji,siq->sjq", flattened, matrices.astype(jnp.float32), precision=FULL_PRECISION)
        return image_rows.reshape(N_SUB, CASES, 4, PAIR).transpose(0, 2, 1, 3)

    def apply_schur(direction):
        operand = (sign_live * direction).astype(jnp.bfloat16)
        image_rows = lax.map(cluster_apply, (schur, operand))
        return jump_rows(image_rows)

    multipliers = jnp.zeros_like(load)
    residual = dual_rhs
    direction = jnp.zeros_like(load)
    rho_old = jnp.ones((CASES,), jnp.float32)
    for iteration in range(ITERS):
        projected = project(residual)
        precond = project(weight * projected)
        rho_now = inner_dot(projected, precond)
        if iteration == 0:
            direction = precond
        else:
            direction = precond + (rho_now / rho_old)[:, None] * direction
        image_rows = apply_schur(direction)
        step_size = rho_now / inner_dot(direction, image_rows)
        multipliers = multipliers + step_size[:, None] * direction
        residual = residual - step_size[:, None] * image_rows
        rho_old = rho_now
    return multipliers, residual
```

```python
import functools

import jax
import jax.numpy as jnp
from jax import lax
from jax.experimental import pallas as pl
from jax.experimental.pallas import tpu as pltpu
from jax.sharding import PartitionSpec as P

MESH = pl.DeviceIdType.MESH
HIGHEST = lax.Precision.HIGHEST
F32 = jnp.float32

NCL, NSUB, CHIPS = 64, 16, 32
CASES, MODES, PAIR = 16, 6, 128
ROWS = 4 * PAIR
SIGNS = (-1.0, 1.0, -1.0, 1.0)


def nn(a, b):
    return lax.dot_general(a, b, (((1,), (0,)), ((), ())), precision=HIGHEST, preferred_element_type=F32)


def nt(a, b):
    return lax.dot_general(a, b, (((1,), (1,)), ((), ())), precision=HIGHEST, preferred_element_type=F32)


def tn(a, b):
    return lax.dot_general(a, b, (((0,), (0,)), ((), ())), precision=HIGHEST, preferred_element_type=F32)


def iota(shape, dim):
    return lax.broadcasted_iota(jnp.int32, shape, dim)


def join(parts):
    return jnp.concatenate(parts, axis=1)


def tile4(x):
    return join([x, x, x, x])


def kernel(
    schur_ref, load_ref, rigid_ref, len_ref, partner_ref, inv_ref, mult_ref, res_ref,
    mat, inv, padded, coupling, edge, edge_in, halo, halo_in, halo2, halo2_in,
    out1, z1_in, g1, out2, z2_in, g2, out3, z3_in, mid3, x3_in, core3, core3_in,
    in_sem, halo_send, halo_recv, tree_send, tree_recv,
):
    c, s = lax.axis_index("clus"), lax.axis_index("sub")
    core, chip = lax.rem(c, 2), lax.div(c, 2)

    z_peers = [(c, lax.rem(s + o, NSUB)) for o in range(1, NSUB)]
    plane = [(lax.rem(chip + o, CHIPS) * 2 + core, s) for o in range(1, CHIPS)]
    other = (chip * 2 + 1 - core, s)
    near = [
        (c, lax.rem(s + NSUB - 1, NSUB)),
        (c, lax.rem(s + 1, NSUB)),
        (lax.rem(c + NCL - 1, NCL), s),
        (lax.rem(c + 1, NCL), s),
    ]
    away = (lax.rem(c + NCL - 1 + 2 * core, NCL), s)
    greeted = z_peers + plane + [other, away]

    barrier = pltpu.get_barrier_semaphore()
    for peer in greeted:
        pl.semaphore_signal(barrier, inc=1, device_id=peer, device_id_type=MESH)

    loads = [
        pltpu.make_async_copy(schur_ref.at[0, 0], mat, in_sem.at[0]),
        pltpu.make_async_copy(load_ref.at[0, 0], edge.at[:, pl.ds(0, CASES)], in_sem.at[1]),
        pltpu.make_async_copy(rigid_ref.at[0, 0], edge.at[:, pl.ds(CASES, MODES)], in_sem.at[2]),
        pltpu.make_async_copy(inv_ref, inv, in_sem.at[3]),
    ]
    for copy in loads:
        copy.start()

    def send_all(src, dst_of, peers, stage):
        for i, peer in enumerate(peers):
            pltpu.make_async_remote_copy(
                src_ref=src, dst_ref=dst_of(i), send_sem=tree_send.at[stage], recv_sem=tree_recv.at[stage],
                device_id=peer, device_id_type=MESH,
            ).start()

    def whole(ref, stage, peer):
        return pltpu.make_async_remote_copy(
            src_ref=ref, dst_ref=ref, send_sem=tree_send.at[stage], recv_sem=tree_recv.at[stage],
            device_id=peer, device_id_type=MESH,
        )

    def halo_copies(src, dst, which):
        return [
            pltpu.make_async_remote_copy(
                src_ref=src.at[d], dst_ref=dst.at[d ^ 1], send_sem=halo_send.at[which, d],
                recv_sem=halo_recv.at[which, d ^ 1], device_id=near[d], device_id_type=MESH,
            )
            for d in range(4)
        ]

    coupling[...] = jnp.zeros((512, 512), F32)
    lane = iota((1, PAIR), 1)
    live_parts = [(lane < len_ref[0, 0, d]).astype(F32) for d in range(4)]
    live = join(live_parts)
    sign_live = join([SIGNS[d] * live_parts[d] for d in range(4)])
    index = [partner_ref[0, 0, pl.ds(d, 1), :] for d in range(4)]

    def partner_rows(x, d):
        return jnp.take_along_axis(x, jnp.broadcast_to(index[d], x.shape), axis=1)

    loads[0].wait()
    eye = iota((PAIR, PAIR), 0) == iota((PAIR, PAIR), 1)
    for d in range(4):
        block = mat[pl.ds(d * PAIR, PAIR), pl.ds(d * PAIR, PAIR)].astype(F32)
        diag = jnp.sum(jnp.where(eye, block, 0.0), axis=0, keepdims=True)
        edge[d, pl.ds(CASES + MODES, 2), :] = jnp.concatenate([diag, jnp.zeros((1, PAIR), F32)], axis=0)
    loads[1].wait()
    loads[2].wait()
    loads[3].wait()
    spread_row, spread_col = iota((512, 384), 0), iota((512, 384), 1)
    slot = spread_row & 7
    spread = jnp.where((slot < MODES) & ((spread_row >> 3) * MODES + slot == spread_col), 1.0, 0.0).astype(F32)
    padded[pl.ds(0, 8), :] = jnp.zeros((8, 512), F32)
    padded[pl.ds(520, 8), :] = jnp.zeros((8, 512), F32)
    padded[pl.ds(8, 512), :] = nt(nn(spread, inv[...]), spread)

    pl.semaphore_wait(barrier, len(greeted))
    edge_copies = halo_copies(edge, edge_in, 0)
    for copy in edge_copies:
        copy.start()

    mode_row = iota((8, PAIR), 0) < MODES
    own = [edge[d] for d in range(4)]
    own_load = join([x[0:CASES] for x in own])
    own_rigid = join([jnp.where(mode_row, x[CASES:], 0.0) for x in own])
    own_diag = join([x[CASES + MODES : CASES + MODES + 1] for x in own])
    signed_rigid = sign_live * own_rigid
    inv3 = padded[pl.ds(pl.multiple_of(c * 8, 8), 24), :]

    for copy in edge_copies:
        copy.wait_recv()
    met = [partner_rows(edge_in[d], d) for d in range(4)]
    far_load = join([x[0:CASES] for x in met])
    far_rigid = [jnp.where(mode_row, x[CASES:], 0.0) for x in met]
    far_diag = join([x[CASES + MODES : CASES + MODES + 1] for x in met])
    weight = jnp.where(live > 0.0, 1.0 / (own_diag + far_diag), 0.0)
    nil = jnp.zeros((8, PAIR), F32)
    rhs = sign_live * (own_load - far_load)
    spread_own = sign_live * (own_rigid - join([far_rigid[0], far_rigid[1], nil, nil]))
    spread_low = -sign_live * join([nil, nil, far_rigid[2], nil])
    spread_high = -sign_live * join([nil, nil, nil, far_rigid[3]])
    basis = jnp.concatenate([spread_low, spread_own, spread_high], axis=0)

    weighted_rhs = weight * rhs
    first = jnp.concatenate([rhs, weighted_rhs, weight * basis, jnp.zeros((72, ROWS), F32)], axis=0)
    sums = nt(signed_rigid, first)
    row8 = iota((8, PAIR), 0)
    packed = sums + pltpu.roll(pltpu.roll(sums, 64, 1), 5, 0)
    out1[...] = packed[0:3]
    send_all(out1, lambda i: z1_in.at[i, pl.ds(0, 3)], z_peers, 0)
    wide1 = sign_live * basis
    signed3 = jnp.concatenate(
        [part for k in range(3) for part in (wide1[8 * k : 8 * k + 8], weight * wide1[8 * k : 8 * k + 8])], axis=0
    )
    whole(z1_in.at[:, pl.ds(0, 3)], 0, z_peers[0]).wait_recv()
    total = out1[...]
    for i in range(NSUB - 1):
        total = total + z1_in[i, pl.ds(0, 3), :]
    g1[core, chip, pl.ds(0, 3), :] = total
    mine1 = g1.at[core, chip, pl.ds(0, 3)]
    send_all(mine1, lambda i: mine1, plane, 1)
    rest1 = g1.at[core, pl.ds(0, CHIPS - 1), pl.ds(0, 3)]
    whole(rest1, 1, plane[0]).wait_recv()
    half1 = g1.at[core, :, pl.ds(0, 3)]
    send_all(half1, lambda i: half1, [other], 2)
    whole(half1, 2, other).wait_recv()

    lane8 = iota((8, PAIR), 1)
    stacked = []
    for k in range(NCL):
        part = jnp.concatenate([g1[k % 2, k // 2, pl.ds(0, 3), :], jnp.zeros((5, PAIR), F32)], axis=0)
        part = part + pltpu.roll(pltpu.roll(part, 64, 1), 3, 0)
        stacked.append(part)
        column = 8 * (k - 1)
        moved = pltpu.roll(part, (column - 32) % PAIR, 1)
        tiles = sorted({(column + 8 * e) // PAIR for e in range(3) if 0 <= k - 1 + e < NCL})
        for t in tiles:
            first_lane = max(column, 0) - t * PAIR
            last_lane = min(column + 24, ROWS) - t * PAIR
            keep = (lane8 >= first_lane) & (lane8 < last_lane)
            coupling[pl.ds(8 * k, 8), pl.ds(t * PAIR, PAIR)] = jnp.where(keep, moved, 0.0)
    gathered = jnp.concatenate(stacked, axis=0)
    twice = nn(nn(inv3, coupling[...]), padded[pl.ds(8, 512), :])
    solver = jnp.concatenate([inv3, twice], axis=0)

    def solve(sums512):
        y = nn(solver, sums512)
        return join([y[0:24, 0:CASES], y[0:24, CASES : 2 * CASES] - y[24:48, 0:CASES]])

    def project(vector, coeffs):
        e = tn(coeffs, basis)
        projected = vector - e[0:CASES]
        return projected, weight * projected - e[CASES:]

    projected, direction = project(rhs, solve(gathered))
    ones = jnp.ones((8, ROWS), F32)
    operand = sign_live * direction
    image = jnp.dot(operand.astype(jnp.bfloat16), mat[...], preferred_element_type=F32)

    image_sums = nt(signed3, image)
    scalars = nt(ones, jnp.concatenate([0.5 * projected * direction, operand * image], axis=0))
    lanes2 = join([image_sums[8 * k : 8 * k + 8] for k in range(6)] + [scalars])
    out2[...] = lanes2[0:6]
    send_all(out2, lambda i: z2_in.at[i, pl.ds(0, 6)], z_peers, 3)
    for d in range(4):
        halo[d] = image[:, d * PAIR : (d + 1) * PAIR]
    image_copies = halo_copies(halo, halo_in, 1)
    for copy in image_copies:
        copy.start()
    whole(z2_in.at[:, pl.ds(0, 6)], 3, z_peers[0]).wait_recv()
    total = out2[...]
    for i in range(NSUB - 1):
        total = total + z2_in[i, pl.ds(0, 6), :]
    g2[core, chip, pl.ds(0, 6), :] = total
    mine2 = g2.at[core, chip, pl.ds(0, 6)]
    send_all(mine2, lambda i: mine2, plane, 4)
    for copy in image_copies:
        copy.wait_recv()
    applied = sign_live * (image - join([partner_rows(halo_in[d], d) for d in range(4)]))
    rest2 = g2.at[core, pl.ds(0, CHIPS - 1), pl.ds(0, 6)]
    whole(rest2, 4, plane[0]).wait_recv()
    half2 = g2.at[core, :, pl.ds(0, 6)]
    send_all(half2, lambda i: half2, [other], 5)
    whole(half2, 5, other).wait_recv()

    parts = [
        jnp.concatenate([g2[k % 2, k // 2, pl.ds(0, 6), :], jnp.zeros((2, PAIR), F32)], axis=0) for k in range(NCL)
    ]
    shifted = []
    for k in range(NCL):
        x = pltpu.roll(parts[k], PAIR - 32, 1)
        if k + 1 < NCL:
            x = x + parts[k + 1]
        if k > 0:
            x = x + pltpu.roll(parts[k - 1], PAIR - 64, 1)
        shifted.append(x)
    sums_all = parts[0]
    for k in range(1, NCL):
        sums_all = sums_all + parts[k]

    def column(row, start, count):
        pick = jnp.where(iota((count * CASES, PAIR), 1) == iota((count * CASES, PAIR), 0) + start, 1.0, 0.0)
        return nt(pick.astype(F32), jnp.broadcast_to(row, (PAIR, PAIR)))

    both = column(sums_all[0:1], 96, 2)
    rho, curve = both[0:CASES], both[CASES:]
    step = tile4(rho / curve)
    projected_f, direction_f = project(applied, solve(jnp.concatenate(shifted, axis=0)))
    projected1 = projected - step * projected_f
    precond1 = direction - step * direction_f
    operand1 = sign_live * precond1
    high = operand1.astype(jnp.bfloat16)
    low = (operand1 - high.astype(F32)).astype(jnp.bfloat16)
    image2 = jnp.dot(jnp.concatenate([high, low], axis=0), mat[...], preferred_element_type=F32)
    image1 = image2[0:CASES] + image2[CASES:]

    scalars3 = nt(
        ones,
        jnp.concatenate(
            [
                0.5 * projected1 * precond1,
                operand1 * image1,
                operand1 * image + operand * image1,
                jnp.zeros((80, ROWS), F32),
            ],
            axis=0,
        ),
    )
    out3[...] = scalars3[0:1]
    send_all(out3, lambda i: z3_in.at[pl.ds(i, 1)], z_peers, 6)
    for d in range(4):
        halo2[d] = image1[:, d * PAIR : (d + 1) * PAIR]
    image_copies1 = halo_copies(halo2, halo2_in, 2)
    for copy in image_copies1:
        copy.start()
    multipliers = step * direction
    residual1 = rhs - step * applied
    whole(z3_in, 6, z_peers[0]).wait_recv()
    mid3[...] = out3[...] + jnp.sum(z3_in[...], axis=0, keepdims=True)
    send_all(mid3, lambda i: x3_in.at[pl.ds(i, 1)], plane, 7)
    for copy in image_copies1:
        copy.wait_recv()
    applied1 = sign_live * (image1 - join([partner_rows(halo2_in[d], d) for d in range(4)]))
    whole(x3_in, 7, plane[0]).wait_recv()
    core3[...] = mid3[...] + jnp.sum(x3_in[...], axis=0, keepdims=True)
    send_all(core3, lambda i: core3_in, [other], 8)
    whole(core3_in, 8, other).wait_recv()
    tail = column(core3[...] + core3_in[...], 0, 3)
    rho1, square, cross = tail[0:CASES], tail[CASES : 2 * CASES], tail[2 * CASES :]
    beta = rho1 / rho
    step1 = tile4(rho1 / (square + beta * cross + beta * beta * curve))
    beta = tile4(beta)
    multipliers = multipliers + step1 * (precond1 + beta * direction)
    residual = residual1 - step1 * (applied1 + beta * applied)
    for d in range(4):
        mult_ref[0, 0, d] = multipliers[:, d * PAIR : (d + 1) * PAIR]
        res_ref[0, 0, d] = residual[:, d * PAIR : (d + 1) * PAIR]

    for copy in edge_copies + image_copies + image_copies1:
        copy.wait_send()
    whole(z1_in.at[:, pl.ds(0, 3)], 0, z_peers[0]).wait_send()
    whole(rest1, 1, plane[0]).wait_send()
    whole(half1, 2, other).wait_send()
    whole(z2_in.at[:, pl.ds(0, 6)], 3, z_peers[0]).wait_send()
    whole(rest2, 4, plane[0]).wait_send()
    whole(half2, 5, other).wait_send()
    whole(z3_in, 6, z_peers[0]).wait_send()
    whole(x3_in, 7, plane[0]).wait_send()
    whole(core3_in, 8, other).wait_send()


def shards(schur, load, rigid, lengths, partner, coarse_inverse):
    anywhere = pl.BlockSpec(memory_space=pl.ANY)
    vmem = pl.BlockSpec(memory_space=pltpu.VMEM)
    out = jax.ShapeDtypeStruct(load.shape, F32)
    return pl.pallas_call(
        kernel,
        out_shape=(out, out),
        in_specs=[anywhere, anywhere, anywhere, pl.BlockSpec(memory_space=pltpu.SMEM), vmem, anywhere],
        out_specs=(vmem, vmem),
        scratch_shapes=[
            pltpu.VMEM((ROWS, ROWS), jnp.bfloat16),
            pltpu.VMEM((384, 384), F32),
            pltpu.VMEM((528, 512), F32),
            pltpu.VMEM((512, 512), F32),
            pltpu.VMEM((4, 24, PAIR), F32),
            pltpu.VMEM((4, 24, PAIR), F32),
            pltpu.VMEM((4, CASES, PAIR), F32),
            pltpu.VMEM((4, CASES, PAIR), F32),
            pltpu.VMEM((4, CASES, PAIR), F32),
            pltpu.VMEM((4, CASES, PAIR), F32),
            pltpu.VMEM((3, PAIR), F32),
            pltpu.VMEM((NSUB - 1, 8, PAIR), F32),
            pltpu.VMEM((2, CHIPS, 8, PAIR), F32),
            pltpu.VMEM((6, PAIR), F32),
            pltpu.VMEM((NSUB - 1, 8, PAIR), F32),
            pltpu.VMEM((2, CHIPS, 8, PAIR), F32),
            pltpu.VMEM((1, PAIR), F32),
            pltpu.VMEM((NSUB - 1, PAIR), F32),
            pltpu.VMEM((1, PAIR), F32),
            pltpu.VMEM((CHIPS - 1, PAIR), F32),
            pltpu.VMEM((1, PAIR), F32),
            pltpu.VMEM((1, PAIR), F32),
            pltpu.SemaphoreType.DMA((4,)),
            pltpu.SemaphoreType.DMA((3, 4)),
            pltpu.SemaphoreType.DMA((3, 4)),
            pltpu.SemaphoreType.DMA((9,)),
            pltpu.SemaphoreType.DMA((9,)),
        ],
        compiler_params=pltpu.CompilerParams(
            collective_id=0, has_side_effects=True, vmem_limit_bytes=32 * 1024 * 1024
        ),
        name="feti",
    )(schur, load, rigid, lengths, partner, coarse_inverse)


def solution(mesh):
    in_specs = (
        P("clus", "sub", None, None),
        P("clus", "sub", None, None, None),
        P("clus", "sub", None, None, None),
        P("clus", "sub", None),
        P("clus", "sub", None, None),
        P(),
    )
    out_specs = (P("clus", "sub", None, None, None), P("clus", "sub", None, None, None))
    return jax.shard_map(shards, mesh=mesh, in_specs=in_specs, out_specs=out_specs, check_vma=False)
```

```python
import functools

import jax
import jax.numpy as jnp
from jax import lax
from jax.experimental import pallas as pl
from jax.experimental.pallas import tpu as pltpu
from jax.sharding import PartitionSpec as P

MESH = pl.DeviceIdType.MESH
HIGHEST = lax.Precision.HIGHEST
F32 = jnp.float32

NCL, NSUB, CHIPS = 64, 16, 32
CASES, MODES, PAIR = 16, 6, 128
ROWS = 4 * PAIR
SIGNS = (-1.0, 1.0, -1.0, 1.0)


def nn(a, b):
    return lax.dot_general(a, b, (((1,), (0,)), ((), ())), precision=HIGHEST, preferred_element_type=F32)


def nt(a, b):
    return lax.dot_general(a, b, (((1,), (1,)), ((), ())), precision=HIGHEST, preferred_element_type=F32)


def tn(a, b):
    return lax.dot_general(a, b, (((0,), (0,)), ((), ())), precision=HIGHEST, preferred_element_type=F32)


def iota(shape, dim):
    return lax.broadcasted_iota(jnp.int32, shape, dim)


def join(parts):
    return jnp.concatenate(parts, axis=1)


def tile4(x):
    return join([x, x, x, x])


def kernel(
    schur_ref, load_ref, rigid_ref, len_ref, partner_ref, inv_ref, both_ref,
    mat, inv, used, rows_of, padded, coupling, edge, edge_in, halo, halo_in, halo2, halo2_in,
    out1, z1_in, g1, out2, z2_in, g2, out3, z3_in, mid3, x3_in, core3, core3_in,
    in_sem, halo_send, halo_recv, tree_send, tree_recv,
):
    c, s = lax.axis_index("clus"), lax.axis_index("sub")
    core, chip = lax.rem(c, 2), lax.div(c, 2)

    z_peers = [(c, lax.rem(s + o, NSUB)) for o in sorted(range(1, NSUB), key=lambda o: -min(o, NSUB - o))]
    y, x = lax.div(chip, 4), lax.rem(chip, 4)
    steps = sorted(range(1, CHIPS), key=lambda o: -(min(o // 4, 8 - o // 4) + min(o % 4, 4 - o % 4)))
    plane = [((lax.rem(y + o // 4, 8) * 4 + lax.rem(x + o % 4, 4)) * 2 + core, s) for o in steps]
    other = (chip * 2 + 1 - core, s)
    near = [
        (c, lax.rem(s + NSUB - 1, NSUB)),
        (c, lax.rem(s + 1, NSUB)),
        (lax.rem(c + NCL - 1, NCL), s),
        (lax.rem(c + 1, NCL), s),
    ]
    away = (lax.rem(c + NCL - 1 + 2 * core, NCL), s)
    greeted = z_peers + plane + [other, away]

    barrier = pltpu.get_barrier_semaphore()
    for peer in greeted:
        pl.semaphore_signal(barrier, inc=1, device_id=peer, device_id_type=MESH)

    loads = [
        pltpu.make_async_copy(load_ref.at[0, 0], edge.at[:, pl.ds(0, CASES)], in_sem.at[0]),
        pltpu.make_async_copy(schur_ref.at[0, 0], mat, in_sem.at[1]),
        pltpu.make_async_copy(len_ref.at[0], used, in_sem.at[2]),
        pltpu.make_async_copy(partner_ref.at[0, 0], rows_of, in_sem.at[3]),
        pltpu.make_async_copy(inv_ref, inv, in_sem.at[4]),
    ] + [
        pltpu.make_async_copy(rigid_ref.at[0, 0, :, d], edge.at[d, pl.ds(CASES, MODES)], in_sem.at[5 + d])
        for d in range(4)
    ]
    for copy in loads[0:2] + loads[5:] + loads[2:5]:
        copy.start()

    def send_all(src, dst_of, peers, stage):
        for i, peer in enumerate(peers):
            pltpu.make_async_remote_copy(
                src_ref=src, dst_ref=dst_of(i), send_sem=tree_send.at[stage], recv_sem=tree_recv.at[stage],
                device_id=peer, device_id_type=MESH,
            ).start()

    def whole(ref, stage, peer):
        return pltpu.make_async_remote_copy(
            src_ref=ref, dst_ref=ref, send_sem=tree_send.at[stage], recv_sem=tree_recv.at[stage],
            device_id=peer, device_id_type=MESH,
        )

    def halo_copies(src, dst, which):
        return [
            pltpu.make_async_remote_copy(
                src_ref=src.at[d], dst_ref=dst.at[d ^ 1], send_sem=halo_send.at[which, d],
                recv_sem=halo_recv.at[which, d ^ 1], device_id=near[d], device_id_type=MESH,
            )
            for d in range(4)
        ]

    loads[1].wait()
    eye = iota((PAIR, PAIR), 0) == iota((PAIR, PAIR), 1)
    for d in range(4):
        block = mat[pl.ds(d * PAIR, PAIR), pl.ds(d * PAIR, PAIR)].astype(F32)
        diag = jnp.sum(jnp.where(eye, block, 0.0), axis=0, keepdims=True)
        edge[d, pl.ds(CASES + MODES, 2), :] = jnp.concatenate([diag, jnp.zeros((1, PAIR), F32)], axis=0)
    for copy in loads[0:1] + loads[5:]:
        copy.wait()
    pl.semaphore_wait(barrier, len(greeted))
    edge_copies = halo_copies(edge, edge_in, 0)
    for copy in edge_copies:
        copy.start()

    for copy in loads[2:4]:
        copy.wait()
    lane = iota((1, PAIR), 1)
    live_parts = [(lane < jnp.broadcast_to(used[:, d : d + 1], (1, PAIR))).astype(F32) for d in range(4)]
    live = join(live_parts)
    sign_live = join([SIGNS[d] * live_parts[d] for d in range(4)])
    index = [rows_of[pl.ds(d, 1), :] for d in range(4)]

    def partner_rows(x, d):
        return jnp.take_along_axis(x, jnp.broadcast_to(index[d], x.shape), axis=1)

    coupling[...] = jnp.zeros((512, 512), F32)
    mode_row = iota((8, PAIR), 0) < MODES
    own = [edge[d] for d in range(4)]
    own_load = join([x[0:CASES] for x in own])
    own_rigid = join([jnp.where(mode_row, x[CASES:], 0.0) for x in own])
    own_diag = join([x[CASES + MODES : CASES + MODES + 1] for x in own])
    signed_rigid = sign_live * own_rigid

    for copy in edge_copies:
        copy.wait_recv()
    met = [partner_rows(edge_in[d], d) for d in range(4)]
    far_load = join([x[0:CASES] for x in met])
    far_rigid = [jnp.where(mode_row, x[CASES:], 0.0) for x in met]
    far_diag = join([x[CASES + MODES : CASES + MODES + 1] for x in met])
    weight = jnp.where(live > 0.0, 1.0 / (own_diag + far_diag), 0.0)
    nil = jnp.zeros((8, PAIR), F32)
    rhs = sign_live * (own_load - far_load)
    spread_own = sign_live * (own_rigid - join([far_rigid[0], far_rigid[1], nil, nil]))
    spread_low = -sign_live * join([nil, nil, far_rigid[2], nil])
    spread_high = -sign_live * join([nil, nil, nil, far_rigid[3]])
    basis = jnp.concatenate([spread_low, spread_own, spread_high], axis=0)

    weighted_rhs = weight * rhs
    first = jnp.concatenate([rhs, weighted_rhs, weight * basis, jnp.zeros((72, ROWS), F32)], axis=0)
    sums = nt(signed_rigid, first)
    row8 = iota((8, PAIR), 0)
    packed = sums + pltpu.roll(pltpu.roll(sums, 64, 1), 5, 0)
    out1[...] = packed[0:3]
    send_all(out1, lambda i: z1_in.at[i, pl.ds(0, 3)], z_peers, 0)
    wide1 = sign_live * basis
    signed3 = jnp.concatenate(
        [part for k in range(3) for part in (wide1[8 * k : 8 * k + 8], weight * wide1[8 * k : 8 * k + 8])], axis=0
    )
    loads[4].wait()
    spread_row, spread_col = iota((512, 384), 0), iota((512, 384), 1)
    slot = spread_row & 7
    spread = jnp.where((slot < MODES) & ((spread_row >> 3) * MODES + slot == spread_col), 1.0, 0.0).astype(F32)
    padded[pl.ds(0, 8), :] = jnp.zeros((8, 512), F32)
    padded[pl.ds(520, 8), :] = jnp.zeros((8, 512), F32)
    padded[pl.ds(8, 512), :] = nt(nn(spread, inv[...]), spread)
    inv3 = padded[pl.ds(pl.multiple_of(c * 8, 8), 24), :]
    whole(z1_in.at[:, pl.ds(0, 3)], 0, z_peers[0]).wait_recv()
    total = out1[...]
    for i in range(NSUB - 1):
        total = total + z1_in[i, pl.ds(0, 3), :]
    g1[core, chip, pl.ds(0, 3), :] = total
    mine1 = g1.at[core, chip, pl.ds(0, 3)]
    send_all(mine1, lambda i: mine1, plane, 1)
    rest1 = g1.at[core, pl.ds(0, CHIPS - 1), pl.ds(0, 3)]
    whole(rest1, 1, plane[0]).wait_recv()
    half1 = g1.at[core, :, pl.ds(0, 3)]
    send_all(half1, lambda i: half1, [other], 2)
    whole(half1, 2, other).wait_recv()

    lane8 = iota((8, PAIR), 1)
    stacked = []
    for k in range(NCL):
        part = jnp.concatenate([g1[k % 2, k // 2, pl.ds(0, 3), :], jnp.zeros((5, PAIR), F32)], axis=0)
        part = part + pltpu.roll(pltpu.roll(part, 64, 1), 3, 0)
        stacked.append(part)
        column = 8 * (k - 1)
        moved = pltpu.roll(part, (column - 32) % PAIR, 1)
        tiles = sorted({(column + 8 * e) // PAIR for e in range(3) if 0 <= k - 1 + e < NCL})
        for t in tiles:
            first_lane = max(column, 0) - t * PAIR
            last_lane = min(column + 24, ROWS) - t * PAIR
            keep = (lane8 >= first_lane) & (lane8 < last_lane)
            coupling[pl.ds(8 * k, 8), pl.ds(t * PAIR, PAIR)] = jnp.where(keep, moved, 0.0)
    gathered = jnp.concatenate(stacked, axis=0)
    twice = nn(nn(inv3, coupling[...]), padded[pl.ds(8, 512), :])
    solver = jnp.concatenate([inv3, twice], axis=0)

    def solve(sums512):
        y = nn(solver, sums512)
        return join([y[0:24, 0:CASES], y[0:24, CASES : 2 * CASES] - y[24:48, 0:CASES]])

    def project(vector, coeffs):
        e = tn(coeffs, basis)
        projected = vector - e[0:CASES]
        return projected, weight * projected - e[CASES:]

    projected, direction = project(rhs, solve(gathered))
    ones = jnp.ones((8, ROWS), F32)
    operand = sign_live * direction
    image = jnp.dot(operand.astype(jnp.bfloat16), mat[...], preferred_element_type=F32)

    image_sums = nt(signed3, image)
    scalars = nt(ones, jnp.concatenate([0.5 * projected * direction, operand * image], axis=0))
    lanes2 = join([image_sums[8 * k : 8 * k + 8] for k in range(6)] + [scalars])
    out2[...] = lanes2[0:6]
    send_all(out2, lambda i: z2_in.at[i, pl.ds(0, 6)], z_peers, 3)
    for d in range(4):
        halo[d] = image[:, d * PAIR : (d + 1) * PAIR]
    image_copies = halo_copies(halo, halo_in, 1)
    for copy in image_copies:
        copy.start()
    whole(z2_in.at[:, pl.ds(0, 6)], 3, z_peers[0]).wait_recv()
    total = out2[...]
    for i in range(NSUB - 1):
        total = total + z2_in[i, pl.ds(0, 6), :]
    g2[core, chip, pl.ds(0, 6), :] = total
    mine2 = g2.at[core, chip, pl.ds(0, 6)]
    send_all(mine2, lambda i: mine2, plane, 4)
    for copy in image_copies:
        copy.wait_recv()
    applied = sign_live * (image - join([partner_rows(halo_in[d], d) for d in range(4)]))
    rest2 = g2.at[core, pl.ds(0, CHIPS - 1), pl.ds(0, 6)]
    whole(rest2, 4, plane[0]).wait_recv()
    half2 = g2.at[core, :, pl.ds(0, 6)]
    send_all(half2, lambda i: half2, [other], 5)
    whole(half2, 5, other).wait_recv()

    parts = [
        jnp.concatenate([g2[k % 2, k // 2, pl.ds(0, 6), :], jnp.zeros((2, PAIR), F32)], axis=0) for k in range(NCL)
    ]
    shifted = []
    for k in range(NCL):
        x = pltpu.roll(parts[k], PAIR - 32, 1)
        if k + 1 < NCL:
            x = x + parts[k + 1]
        if k > 0:
            x = x + pltpu.roll(parts[k - 1], PAIR - 64, 1)
        shifted.append(x)
    sums_all = parts[0]
    for k in range(1, NCL):
        sums_all = sums_all + parts[k]

    def column(row, start, count):
        pick = jnp.where(iota((count * CASES, PAIR), 1) == iota((count * CASES, PAIR), 0) + start, 1.0, 0.0)
        return nt(pick.astype(F32), jnp.broadcast_to(row, (PAIR, PAIR)))

    both = column(sums_all[0:1], 96, 2)
    rho, curve = both[0:CASES], both[CASES:]
    step = tile4(rho / curve)
    projected_f, direction_f = project(applied, solve(jnp.concatenate(shifted, axis=0)))
    projected1 = projected - step * projected_f
    precond1 = direction - step * direction_f
    operand1 = sign_live * precond1
    high = operand1.astype(jnp.bfloat16)
    low = (operand1 - high.astype(F32)).astype(jnp.bfloat16)
    image2 = jnp.dot(jnp.concatenate([high, low], axis=0), mat[...], preferred_element_type=F32)
    image1 = image2[0:CASES] + image2[CASES:]

    scalars3 = nt(
        ones,
        jnp.concatenate(
            [
                0.5 * projected1 * precond1,
                operand1 * image1,
                operand1 * image + operand * image1,
                jnp.zeros((80, ROWS), F32),
            ],
            axis=0,
        ),
    )
    out3[...] = scalars3[0:1]
    send_all(out3, lambda i: z3_in.at[pl.ds(i, 1)], z_peers, 6)
    for d in range(4):
        halo2[d] = image1[:, d * PAIR : (d + 1) * PAIR]
    image_copies1 = halo_copies(halo2, halo2_in, 2)
    for copy in image_copies1:
        copy.start()
    multipliers = step * direction
    residual1 = rhs - step * applied
    whole(z3_in, 6, z_peers[0]).wait_recv()
    mid3[...] = out3[...] + jnp.sum(z3_in[...], axis=0, keepdims=True)
    send_all(mid3, lambda i: x3_in.at[pl.ds(i, 1)], plane, 7)
    for copy in image_copies1:
        copy.wait_recv()
    applied1 = sign_live * (image1 - join([partner_rows(halo2_in[d], d) for d in range(4)]))
    whole(x3_in, 7, plane[0]).wait_recv()
    core3[...] = mid3[...] + jnp.sum(x3_in[...], axis=0, keepdims=True)
    send_all(core3, lambda i: core3_in, [other], 8)
    whole(core3_in, 8, other).wait_recv()
    tail = column(core3[...] + core3_in[...], 0, 3)
    rho1, square, cross = tail[0:CASES], tail[CASES : 2 * CASES], tail[2 * CASES :]
    beta = rho1 / rho
    step1 = tile4(rho1 / (square + beta * cross + beta * beta * curve))
    beta = tile4(beta)
    multipliers = multipliers + step1 * (precond1 + beta * direction)
    residual = residual1 - step1 * (applied1 + beta * applied)
    for d in range(4):
        both_ref[0, d] = multipliers[:, d * PAIR : (d + 1) * PAIR]
        both_ref[1, d] = residual[:, d * PAIR : (d + 1) * PAIR]

    for copy in edge_copies + image_copies + image_copies1:
        copy.wait_send()
    whole(z1_in.at[:, pl.ds(0, 3)], 0, z_peers[0]).wait_send()
    whole(rest1, 1, plane[0]).wait_send()
    whole(half1, 2, other).wait_send()
    whole(z2_in.at[:, pl.ds(0, 6)], 3, z_peers[0]).wait_send()
    whole(rest2, 4, plane[0]).wait_send()
    whole(half2, 5, other).wait_send()
    whole(z3_in, 6, z_peers[0]).wait_send()
    whole(x3_in, 7, plane[0]).wait_send()
    whole(core3_in, 8, other).wait_send()


def shards(schur, load, rigid, lengths, partner, coarse_inverse):
    hbm = pl.BlockSpec(memory_space=pl.ANY)
    vmem = pl.BlockSpec(memory_space=pltpu.VMEM)
    out = jax.ShapeDtypeStruct((2,) + load.shape[2:], F32)
    both = pl.pallas_call(
        kernel,
        out_shape=out,
        in_specs=[hbm] * 6,
        out_specs=vmem,
        scratch_shapes=[
            pltpu.VMEM((ROWS, ROWS), jnp.bfloat16),
            pltpu.VMEM((384, 384), F32),
            pltpu.VMEM((1, 4), jnp.int32),
            pltpu.VMEM((4, PAIR), jnp.int32),
            pltpu.VMEM((528, 512), F32),
            pltpu.VMEM((512, 512), F32),
            pltpu.VMEM((4, 24, PAIR), F32),
            pltpu.VMEM((4, 24, PAIR), F32),
            pltpu.VMEM((4, CASES, PAIR), F32),
            pltpu.VMEM((4, CASES, PAIR), F32),
            pltpu.VMEM((4, CASES, PAIR), F32),
            pltpu.VMEM((4, CASES, PAIR), F32),
            pltpu.VMEM((3, PAIR), F32),
            pltpu.VMEM((NSUB - 1, 8, PAIR), F32),
            pltpu.VMEM((2, CHIPS, 8, PAIR), F32),
            pltpu.VMEM((6, PAIR), F32),
            pltpu.VMEM((NSUB - 1, 8, PAIR), F32),
            pltpu.VMEM((2, CHIPS, 8, PAIR), F32),
            pltpu.VMEM((1, PAIR), F32),
            pltpu.VMEM((NSUB - 1, PAIR), F32),
            pltpu.VMEM((1, PAIR), F32),
            pltpu.VMEM((CHIPS - 1, PAIR), F32),
            pltpu.VMEM((1, PAIR), F32),
            pltpu.VMEM((1, PAIR), F32),
            pltpu.SemaphoreType.DMA((9,)),
            pltpu.SemaphoreType.DMA((3, 4)),
            pltpu.SemaphoreType.DMA((3, 4)),
            pltpu.SemaphoreType.DMA((9,)),
            pltpu.SemaphoreType.DMA((9,)),
        ],
        compiler_params=pltpu.CompilerParams(
            collective_id=0, has_side_effects=True, vmem_limit_bytes=60 * 1024*1024
        ),
        name="feti",
    )(schur, load, jnp.transpose(rigid, (0, 1, 3, 2, 4)), lengths, partner, coarse_inverse)
    return both[0][None, None], both[1][None, None]


def solution(mesh):
    in_specs = (
        P("clus", "sub", None, None),
        P("clus", "sub", None, None, None),
        P("clus", "sub", None, None, None),
        P("clus", "sub", None),
        P("clus", "sub", None, None),
        P(),
    )
    out_specs = (P("clus", "sub", None, None, None), P("clus", "sub", None, None, None))
    return jax.shard_map(shards, mesh=mesh, in_specs=in_specs, out_specs=out_specs, check_vma=False)
```

```python
import functools

import jax
import jax.numpy as jnp
from jax import lax
from jax.experimental import pallas as pl
from jax.experimental.pallas import tpu as pltpu
from jax.sharding import PartitionSpec as P

MESH = pl.DeviceIdType.MESH
HIGHEST = lax.Precision.HIGHEST
F32 = jnp.float32

NCL, NSUB, CHIPS = 64, 16, 32
CASES, MODES, PAIR = 16, 6, 128
ROWS = 4 * PAIR
SIGNS = (-1.0, 1.0, -1.0, 1.0)


def full_dot(a, b, dims):
    return lax.dot_general(a, b, (dims, ((), ())), precision=HIGHEST, preferred_element_type=F32)


def split(x):
    high = x.astype(jnp.bfloat16).astype(F32)
    return high, x - high


def dot3(a, b, dims):
    keep = 1 - dims[0][0]
    count = a.shape[keep]
    a_high, a_low = split(a)
    pair = jnp.concatenate([a_high, a_low], axis=keep).astype(jnp.bfloat16)
    b_high, b_low = b if isinstance(b, tuple) else [x.astype(jnp.bfloat16) for x in split(b)]

    def dot(x, y):
        return lax.dot_general(x, y, (dims, ((), ())), preferred_element_type=F32)

    both = dot(pair, b_high)
    return both[:count] + both[count:] + dot(a_high.astype(jnp.bfloat16), b_low)


def nn(a, b):
    return dot3(a, b, ((1,), (0,)))


def nt(a, b):
    return dot3(a, b, ((1,), (1,)))


def tn(a, b):
    return dot3(a, b, ((0,), (0,)))


def iota(shape, dim):
    return lax.broadcasted_iota(jnp.int32, shape, dim)


def join(parts):
    return jnp.concatenate(parts, axis=1)


def tile4(x):
    return join([x, x, x, x])


def kernel(
    schur_ref, load_ref, rigid_ref, len_ref, partner_ref, inv_ref, both_ref,
    mat, corner, inv, used, rows_of, padded, padded_high, padded_low, coupling, edge, edge_in, halo, halo_in, halo2, halo2_in,
    out1, z1_in, g1, out2, z2_in, g2, out3, z3_in, mid3, x3_in, core3, core3_in,
    in_sem, halo_send, halo_recv, tree_send, tree_recv, ready,
):
    c, s = lax.axis_index("clus"), lax.axis_index("sub")
    core, chip = lax.rem(c, 2), lax.div(c, 2)

    z_peers = [(c, lax.rem(s + o, NSUB)) for o in sorted(range(1, NSUB), key=lambda o: -min(o, NSUB - o))]
    y, x = lax.div(chip, 4), lax.rem(chip, 4)
    steps = sorted(range(1, CHIPS), key=lambda o: -(min(o // 4, 8 - o // 4) + min(o % 4, 4 - o % 4)))
    plane = [((lax.rem(y + o // 4, 8) * 4 + lax.rem(x + o % 4, 4)) * 2 + core, s) for o in steps]
    other = (chip * 2 + 1 - core, s)
    near = [
        (c, lax.rem(s + NSUB - 1, NSUB)),
        (c, lax.rem(s + 1, NSUB)),
        (lax.rem(c + NCL - 1, NCL), s),
        (lax.rem(c + 1, NCL), s),
    ]
    away = (lax.rem(c + NCL - 1 + 2 * core, NCL), s)

    def z_by(o):
        return (c, lax.rem(s + o + NSUB, NSUB))

    def y_by(o):
        return ((lax.rem(y + o + 8, 8) * 4 + x) * 2 + core, s)

    def x_by(o):
        return ((y * 4 + lax.rem(x + o + 4, 4)) * 2 + core, s)

    greeted = [z_by(-1), z_by(1), y_by(-1), y_by(1), x_by(-1), x_by(1), other, away]
    told = [
        [z_by(-1), z_by(1)],
        [z_by(-2), z_by(2)],
        [z_by(-4), z_by(4)],
        [x_by(-1), x_by(1)],
        [y_by(-1), y_by(1)],
        [y_by(-2), y_by(2)],
        [y_by(-1), y_by(1)],
    ]

    def tell(k):
        for peer in told[k]:
            pl.semaphore_signal(ready.at[k], inc=1, device_id=peer, device_id_type=MESH)

    def hear(k):
        pl.semaphore_wait(ready.at[k], 2)

    barrier = pltpu.get_barrier_semaphore()
    for peer in greeted:
        pl.semaphore_signal(barrier, inc=1, device_id=peer, device_id_type=MESH)

    loads = [
        pltpu.make_async_copy(load_ref.at[0, 0], edge.at[:, pl.ds(0, CASES)], in_sem.at[0]),
        pltpu.make_async_copy(schur_ref.at[0, 0], mat, in_sem.at[1]),
        pltpu.make_async_copy(len_ref.at[0], used, in_sem.at[2]),
        pltpu.make_async_copy(partner_ref.at[0, 0], rows_of, in_sem.at[3]),
        pltpu.make_async_copy(inv_ref, inv, in_sem.at[4]),
    ]
    rigid_loads = [
        pltpu.make_async_copy(rigid_ref.at[0, 0, :, d], edge.at[d, pl.ds(CASES, MODES)], in_sem.at[5 + d])
        for d in range(4)
    ]
    corner_loads = [
        pltpu.make_async_copy(
            schur_ref.at[0, 0, pl.ds(d * PAIR, PAIR), pl.ds(d * PAIR, PAIR)], corner.at[d], in_sem.at[9 + d]
        )
        for d in range(4)
    ]
    for copy in corner_loads + rigid_loads + loads[0:1] + loads[2:4] + loads[1:2] + loads[4:5]:
        copy.start()

    def send_all(src, dst_of, peers, stage):
        for i, peer in enumerate(peers):
            pltpu.make_async_remote_copy(
                src_ref=src, dst_ref=dst_of(i), send_sem=tree_send.at[stage], recv_sem=tree_recv.at[stage],
                device_id=peer, device_id_type=MESH,
            ).start()

    def whole(ref, stage, peer):
        return pltpu.make_async_remote_copy(
            src_ref=ref, dst_ref=ref, send_sem=tree_send.at[stage], recv_sem=tree_recv.at[stage],
            device_id=peer, device_id_type=MESH,
        )

    def halo_copies(src, dst, which):
        return [
            pltpu.make_async_remote_copy(
                src_ref=src.at[d], dst_ref=dst.at[d ^ 1], send_sem=halo_send.at[which, d],
                recv_sem=halo_recv.at[which, d ^ 1], device_id=near[d], device_id_type=MESH,
            )
            for d in range(4)
        ]

    pl.semaphore_wait(barrier, len(greeted))
    tell(0)
    tell(3)
    eye = iota((PAIR, PAIR), 0) == iota((PAIR, PAIR), 1)
    for d in range(4):
        corner_loads[d].wait()
        block = corner[d].astype(F32)
        diag = jnp.sum(jnp.where(eye, block, 0.0), axis=0, keepdims=True)
        edge[d, pl.ds(CASES + MODES, 2), :] = jnp.concatenate([diag, jnp.zeros((1, PAIR), F32)], axis=0)
    for copy in loads[0:1] + rigid_loads:
        copy.wait()
    edge_copies = halo_copies(edge, edge_in, 0)
    for copy in edge_copies:
        copy.start()
    hear(0)
    tell(1)
    hear(3)
    tell(4)

    for copy in loads[2:4]:
        copy.wait()
    lane = iota((1, PAIR), 1)
    live_parts = [(lane < jnp.broadcast_to(used[:, d : d + 1], (1, PAIR))).astype(F32) for d in range(4)]
    live = join(live_parts)
    sign_live = join([SIGNS[d] * live_parts[d] for d in range(4)])
    index = [rows_of[pl.ds(d, 1), :] for d in range(4)]

    def partner_rows(x, d):
        return jnp.take_along_axis(x, jnp.broadcast_to(index[d], x.shape), axis=1)

    coupling[...] = jnp.zeros((512, 512), F32)
    mode_row = iota((8, PAIR), 0) < MODES
    own = [edge[d] for d in range(4)]
    own_load = join([x[0:CASES] for x in own])
    own_rigid = join([jnp.where(mode_row, x[CASES:], 0.0) for x in own])
    own_diag = join([x[CASES + MODES : CASES + MODES + 1] for x in own])
    signed_rigid = sign_live * own_rigid

    hear(1)
    tell(2)
    hear(4)
    tell(5)
    for copy in edge_copies:
        copy.wait_recv()
    met = [partner_rows(edge_in[d], d) for d in range(4)]
    far_load = join([x[0:CASES] for x in met])
    far_rigid = [jnp.where(mode_row, x[CASES:], 0.0) for x in met]
    far_diag = join([x[CASES + MODES : CASES + MODES + 1] for x in met])
    weight = jnp.where(live > 0.0, 1.0 / (own_diag + far_diag), 0.0)
    nil = jnp.zeros((8, PAIR), F32)
    rhs = sign_live * (own_load - far_load)
    spread_own = sign_live * (own_rigid - join([far_rigid[0], far_rigid[1], nil, nil]))
    spread_low = -sign_live * join([nil, nil, far_rigid[2], nil])
    spread_high = -sign_live * join([nil, nil, nil, far_rigid[3]])
    basis = jnp.concatenate([spread_low, spread_own, spread_high], axis=0)

    weighted_rhs = weight * rhs
    first = jnp.concatenate([rhs, weighted_rhs, weight * basis, jnp.zeros((72, ROWS), F32)], axis=0)
    sums = nt(signed_rigid, first)
    row8 = iota((8, PAIR), 0)
    packed = sums + pltpu.roll(pltpu.roll(sums, 64, 1), 5, 0)
    out1[...] = packed[0:3]
    hear(2)
    send_all(out1, lambda i: z1_in.at[i, pl.ds(0, 3)], z_peers, 0)
    wide1 = sign_live * basis
    signed3 = jnp.concatenate(
        [part for k in range(3) for part in (wide1[8 * k : 8 * k + 8], weight * wide1[8 * k : 8 * k + 8])], axis=0
    )
    hear(5)
    tell(6)
    loads[1].wait()
    loads[4].wait()
    spread_row, spread_col = iota((512, 384), 0), iota((512, 384), 1)
    slot = spread_row & 7
    spread = jnp.where((slot < MODES) & ((spread_row >> 3) * MODES + slot == spread_col), 1.0, 0.0).astype(F32)
    padded[pl.ds(0, 8), :] = jnp.zeros((8, 512), F32)
    padded[pl.ds(520, 8), :] = jnp.zeros((8, 512), F32)
    padded[pl.ds(8, 512), :] = full_dot(full_dot(spread, inv[...], ((1,), (0,))), spread, ((1,), (1,)))
    inv3 = padded[pl.ds(pl.multiple_of(c * 8, 8), 24), :]
    padded_high[...], padded_low[...] = [part.astype(jnp.bfloat16) for part in split(padded[pl.ds(8, 512), :])]
    whole(z1_in.at[:, pl.ds(0, 3)], 0, z_peers[0]).wait_recv()
    total = out1[...]
    for i in range(NSUB - 1):
        total = total + z1_in[i, pl.ds(0, 3), :]
    g1[core, chip, pl.ds(0, 3), :] = total
    hear(6)
    mine1 = g1.at[core, chip, pl.ds(0, 3)]
    send_all(mine1, lambda i: mine1, plane, 1)
    rest1 = g1.at[core, pl.ds(0, CHIPS - 1), pl.ds(0, 3)]
    whole(rest1, 1, plane[0]).wait_recv()
    half1 = g1.at[core, :, pl.ds(0, 3)]
    send_all(half1, lambda i: half1, [other], 2)
    whole(half1, 2, other).wait_recv()

    lane8 = iota((8, PAIR), 1)
    stacked = []
    for k in range(NCL):
        part = jnp.concatenate([g1[k % 2, k // 2, pl.ds(0, 3), :], jnp.zeros((5, PAIR), F32)], axis=0)
        part = part + pltpu.roll(pltpu.roll(part, 64, 1), 3, 0)
        stacked.append(part)
        column = 8 * (k - 1)
        moved = pltpu.roll(part, (column - 32) % PAIR, 1)
        tiles = sorted({(column + 8 * e) // PAIR for e in range(3) if 0 <= k - 1 + e < NCL})
        for t in tiles:
            first_lane = max(column, 0) - t * PAIR
            last_lane = min(column + 24, ROWS) - t * PAIR
            keep = (lane8 >= first_lane) & (lane8 < last_lane)
            coupling[pl.ds(8 * k, 8), pl.ds(t * PAIR, PAIR)] = jnp.where(keep, moved, 0.0)
    gathered = jnp.concatenate(stacked, axis=0)
    twice = nn(nn(inv3, coupling[...]), (padded_high[...], padded_low[...]))
    solver = jnp.concatenate([inv3, twice], axis=0)

    def solve(sums512):
        y = nn(solver, sums512)
        return join([y[0:24, 0:CASES], y[0:24, CASES : 2 * CASES] - y[24:48, 0:CASES]])

    def project(vector, coeffs):
        e = tn(coeffs, basis)
        projected = vector - e[0:CASES]
        return projected, weight * projected - e[CASES:]

    projected, direction = project(rhs, solve(gathered))
    ones = jnp.ones((8, ROWS), F32)
    operand = sign_live * direction
    image = jnp.dot(operand.astype(jnp.bfloat16), mat[...], preferred_element_type=F32)

    image_sums = nt(signed3, image)
    scalars = nt(ones, jnp.concatenate([0.5 * projected * direction, operand * image], axis=0))
    lanes2 = join([image_sums[8 * k : 8 * k + 8] for k in range(6)] + [scalars])
    out2[...] = lanes2[0:6]
    send_all(out2, lambda i: z2_in.at[i, pl.ds(0, 6)], z_peers, 3)
    for d in range(4):
        halo[d] = image[:, d * PAIR : (d + 1) * PAIR]
    image_copies = halo_copies(halo, halo_in, 1)
    for copy in image_copies:
        copy.start()
    whole(z2_in.at[:, pl.ds(0, 6)], 3, z_peers[0]).wait_recv()
    total = out2[...]
    for i in range(NSUB - 1):
        total = total + z2_in[i, pl.ds(0, 6), :]
    g2[core, chip, pl.ds(0, 6), :] = total
    mine2 = g2.at[core, chip, pl.ds(0, 6)]
    send_all(mine2, lambda i: mine2, plane, 4)
    for copy in image_copies:
        copy.wait_recv()
    applied = sign_live * (image - join([partner_rows(halo_in[d], d) for d in range(4)]))
    rest2 = g2.at[core, pl.ds(0, CHIPS - 1), pl.ds(0, 6)]
    whole(rest2, 4, plane[0]).wait_recv()
    half2 = g2.at[core, :, pl.ds(0, 6)]
    send_all(half2, lambda i: half2, [other], 5)
    whole(half2, 5, other).wait_recv()

    parts = [
        jnp.concatenate([g2[k % 2, k // 2, pl.ds(0, 6), :], jnp.zeros((2, PAIR), F32)], axis=0) for k in range(NCL)
    ]
    shifted = []
    for k in range(NCL):
        x = pltpu.roll(parts[k], PAIR - 32, 1)
        if k + 1 < NCL:
            x = x + parts[k + 1]
        if k > 0:
            x = x + pltpu.roll(parts[k - 1], PAIR - 64, 1)
        shifted.append(x)
    sums_all = parts[0]
    for k in range(1, NCL):
        sums_all = sums_all + parts[k]

    def column(row, start, count):
        pick = jnp.where(iota((count * CASES, PAIR), 1) == iota((count * CASES, PAIR), 0) + start, 1.0, 0.0)
        return full_dot(pick.astype(F32), jnp.broadcast_to(row, (PAIR, PAIR)), ((1,), (1,)))

    both = column(sums_all[0:1], 96, 2)
    rho, curve = both[0:CASES], both[CASES:]
    step = tile4(rho / curve)
    projected_f, direction_f = project(applied, solve(jnp.concatenate(shifted, axis=0)))
    projected1 = projected - step * projected_f
    precond1 = direction - step * direction_f
    operand1 = sign_live * precond1
    high = operand1.astype(jnp.bfloat16)
    low = (operand1 - high.astype(F32)).astype(jnp.bfloat16)
    image2 = jnp.dot(jnp.concatenate([high, low], axis=0), mat[...], preferred_element_type=F32)
    image1 = image2[0:CASES] + image2[CASES:]

    scalars3 = nt(
        ones,
        jnp.concatenate(
            [
                0.5 * projected1 * precond1,
                operand1 * image1,
                operand1 * image + operand * image1,
                jnp.zeros((80, ROWS), F32),
            ],
            axis=0,
        ),
    )
    out3[...] = scalars3[0:1]
    send_all(out3, lambda i: z3_in.at[pl.ds(i, 1)], z_peers, 6)
    for d in range(4):
        halo2[d] = image1[:, d * PAIR : (d + 1) * PAIR]
    image_copies1 = halo_copies(halo2, halo2_in, 2)
    for copy in image_copies1:
        copy.start()
    multipliers = step * direction
    residual1 = rhs - step * applied
    whole(z3_in, 6, z_peers[0]).wait_recv()
    mid3[...] = out3[...] + jnp.sum(z3_in[...], axis=0, keepdims=True)
    send_all(mid3, lambda i: x3_in.at[pl.ds(i, 1)], plane, 7)
    for copy in image_copies1:
        copy.wait_recv()
    applied1 = sign_live * (image1 - join([partner_rows(halo2_in[d], d) for d in range(4)]))
    whole(x3_in, 7, plane[0]).wait_recv()
    core3[...] = mid3[...] + jnp.sum(x3_in[...], axis=0, keepdims=True)
    send_all(core3, lambda i: core3_in, [other], 8)
    whole(core3_in, 8, other).wait_recv()
    tail = column(core3[...] + core3_in[...], 0, 3)
    rho1, square, cross = tail[0:CASES], tail[CASES : 2 * CASES], tail[2 * CASES :]
    beta = rho1 / rho
    step1 = tile4(rho1 / (square + beta * cross + beta * beta * curve))
    beta = tile4(beta)
    multipliers = multipliers + step1 * (precond1 + beta * direction)
    residual = residual1 - step1 * (applied1 + beta * applied)
    for d in range(4):
        both_ref[0, d] = multipliers[:, d * PAIR : (d + 1) * PAIR]
        both_ref[1, d] = residual[:, d * PAIR : (d + 1) * PAIR]

    for copy in edge_copies + image_copies + image_copies1:
        copy.wait_send()
    whole(z1_in.at[:, pl.ds(0, 3)], 0, z_peers[0]).wait_send()
    whole(rest1, 1, plane[0]).wait_send()
    whole(half1, 2, other).wait_send()
    whole(z2_in.at[:, pl.ds(0, 6)], 3, z_peers[0]).wait_send()
    whole(rest2, 4, plane[0]).wait_send()
    whole(half2, 5, other).wait_send()
    whole(z3_in, 6, z_peers[0]).wait_send()
    whole(x3_in, 7, plane[0]).wait_send()
    whole(core3_in, 8, other).wait_send()


def shards(schur, load, rigid, lengths, partner, coarse_inverse):
    hbm = pl.BlockSpec(memory_space=pl.ANY)
    vmem = pl.BlockSpec(memory_space=pltpu.VMEM)
    out = jax.ShapeDtypeStruct((2,) + load.shape[2:], F32)
    both = pl.pallas_call(
        kernel,
        out_shape=out,
        in_specs=[hbm] * 6,
        out_specs=vmem,
        scratch_shapes=[
            pltpu.VMEM((ROWS, ROWS), jnp.bfloat16),
            pltpu.VMEM((4, PAIR, PAIR), jnp.bfloat16),
            pltpu.VMEM((384, 384), F32),
            pltpu.VMEM((1, 4), jnp.int32),
            pltpu.VMEM((4, PAIR), jnp.int32),
            pltpu.VMEM((528, 512), F32),
            pltpu.VMEM((512, 512), jnp.bfloat16),
            pltpu.VMEM((512, 512), jnp.bfloat16),
            pltpu.VMEM((512, 512), F32),
            pltpu.VMEM((4, 24, PAIR), F32),
            pltpu.VMEM((4, 24, PAIR), F32),
            pltpu.VMEM((4, CASES, PAIR), F32),
            pltpu.VMEM((4, CASES, PAIR), F32),
            pltpu.VMEM((4, CASES, PAIR), F32),
            pltpu.VMEM((4, CASES, PAIR), F32),
            pltpu.VMEM((3, PAIR), F32),
            pltpu.VMEM((NSUB - 1, 8, PAIR), F32),
            pltpu.VMEM((2, CHIPS, 8, PAIR), F32),
            pltpu.VMEM((6, PAIR), F32),
            pltpu.VMEM((NSUB - 1, 8, PAIR), F32),
            pltpu.VMEM((2, CHIPS, 8, PAIR), F32),
            pltpu.VMEM((1, PAIR), F32),
            pltpu.VMEM((NSUB - 1, PAIR), F32),
            pltpu.VMEM((1, PAIR), F32),
            pltpu.VMEM((CHIPS - 1, PAIR), F32),
            pltpu.VMEM((1, PAIR), F32),
            pltpu.VMEM((1, PAIR), F32),
            pltpu.SemaphoreType.DMA((13,)),
            pltpu.SemaphoreType.DMA((3, 4)),
            pltpu.SemaphoreType.DMA((3, 4)),
            pltpu.SemaphoreType.DMA((9,)),
            pltpu.SemaphoreType.DMA((9,)),
            pltpu.SemaphoreType.REGULAR((7,)),
        ],
        compiler_params=pltpu.CompilerParams(
            collective_id=0, has_side_effects=True, vmem_limit_bytes=60 * 1024*1024
        ),
        name="feti",
    )(schur, load, jnp.transpose(rigid, (0, 1, 3, 2, 4)), lengths, partner, coarse_inverse)
    return both[0][None, None], both[1][None, None]


def solution(mesh):
    in_specs = (
        P("clus", "sub", None, None),
        P("clus", "sub", None, None, None),
        P("clus", "sub", None, None, None),
        P("clus", "sub", None),
        P("clus", "sub", None, None),
        P(),
    )
    out_specs = (P("clus", "sub", None, None, None), P("clus", "sub", None, None, None))
    return jax.shard_map(shards, mesh=mesh, in_specs=in_specs, out_specs=out_specs, check_vma=False)
```

```python
import functools

import jax
import jax.numpy as jnp
from jax import lax
from jax.experimental import pallas as pl
from jax.experimental.pallas import tpu as pltpu
from jax.sharding import PartitionSpec as P

MESH = pl.DeviceIdType.MESH
HIGHEST = lax.Precision.HIGHEST
F32 = jnp.float32

NCL, NSUB, CHIPS = 64, 16, 32
CASES, MODES, PAIR = 16, 6, 128
ROWS = 4 * PAIR
SIGNS = (-1.0, 1.0, -1.0, 1.0)


def full_dot(a, b, dims):
    return lax.dot_general(a, b, (dims, ((), ())), precision=HIGHEST, preferred_element_type=F32)


def split(x):
    high = x.astype(jnp.bfloat16).astype(F32)
    return high, x - high


def dot3(a, b, dims):
    keep = 1 - dims[0][0]
    count = a.shape[keep]
    a_high, a_low = split(a)
    pair = jnp.concatenate([a_high, a_low], axis=keep).astype(jnp.bfloat16)
    b_high, b_low = b if isinstance(b, tuple) else [x.astype(jnp.bfloat16) for x in split(b)]

    def dot(x, y):
        return lax.dot_general(x, y, (dims, ((), ())), preferred_element_type=F32)

    both = dot(pair, b_high)
    return both[:count] + both[count:] + dot(a_high.astype(jnp.bfloat16), b_low)


def nn(a, b):
    return dot3(a, b, ((1,), (0,)))


def nt(a, b):
    return dot3(a, b, ((1,), (1,)))


def tn(a, b):
    return dot3(a, b, ((0,), (0,)))


def iota(shape, dim):
    return lax.broadcasted_iota(jnp.int32, shape, dim)


def join(parts):
    return jnp.concatenate(parts, axis=1)


def tile4(x):
    return join([x, x, x, x])


def kernel(
    schur_ref, load_ref, rigid_ref, len_ref, partner_ref, inv_ref, terms_ref, step_ref, older_ref, staged,
    mat, corner, inv, used, rows_of, padded, padded_high, padded_low, coupling, edge, edge_in, halo, halo_in, halo2, halo2_in,
    out1, z1_in, g1, out2, z2_in, g2, out3, z3_in, mid3, x3_in,
    in_sem, halo_send, halo_recv, tree_send, tree_recv, ready,
):
    c, s = lax.axis_index("clus"), lax.axis_index("sub")
    core, chip = lax.rem(c, 2), lax.div(c, 2)

    z_peers = [(c, lax.rem(s + o, NSUB)) for o in sorted(range(1, NSUB), key=lambda o: -min(o, NSUB - o))]
    y, x = lax.div(chip, 4), lax.rem(chip, 4)
    steps = sorted(range(1, CHIPS), key=lambda o: -(min(o // 4, 8 - o // 4) + min(o % 4, 4 - o % 4)))
    plane = [((lax.rem(y + o // 4, 8) * 4 + lax.rem(x + o % 4, 4)) * 2 + core, s) for o in steps]
    other = (chip * 2 + 1 - core, s)
    spans = sorted(
        range(1, NCL), key=lambda o: -(min(o // 8, 8 - o // 8) + min(o // 2 % 4, 4 - o // 2 % 4) + o % 2)
    )
    clusters = [
        ((lax.rem(y + o // 8, 8) * 4 + lax.rem(x + o // 2 % 4, 4)) * 2 + lax.rem(core + o % 2, 2), s) for o in spans
    ]
    columns = sorted(range(1, 2 * NSUB), key=lambda o: -(min(o // 2, NSUB - o // 2) + o % 2))
    column_peers = [(chip * 2 + lax.rem(core + o, 2), lax.rem(s + o // 2, NSUB)) for o in columns]
    near = [
        (c, lax.rem(s + NSUB - 1, NSUB)),
        (c, lax.rem(s + 1, NSUB)),
        (lax.rem(c + NCL - 1, NCL), s),
        (lax.rem(c + 1, NCL), s),
    ]
    away = (lax.rem(c + NCL - 1 + 2 * core, NCL), s)

    def z_by(o):
        return (c, lax.rem(s + o + NSUB, NSUB))

    def y_by(o):
        return ((lax.rem(y + o + 8, 8) * 4 + x) * 2 + core, s)

    def x_by(o):
        return ((y * 4 + lax.rem(x + o + 4, 4)) * 2 + core, s)

    greeted = [z_by(-1), z_by(1), y_by(-1), y_by(1), x_by(-1), x_by(1), other, away]
    told = [
        [z_by(-1), z_by(1)],
        [z_by(-2), z_by(2)],
        [z_by(-4), z_by(4)],
        [x_by(-1), x_by(1)],
        [y_by(-1), y_by(1)],
        [y_by(-2), y_by(2)],
        [y_by(-1), y_by(1)],
    ]

    def tell(k):
        for peer in told[k]:
            pl.semaphore_signal(ready.at[k], inc=1, device_id=peer, device_id_type=MESH)

    def hear(k):
        pl.semaphore_wait(ready.at[k], 2)

    barrier = pltpu.get_barrier_semaphore()
    for peer in greeted:
        pl.semaphore_signal(barrier, inc=1, device_id=peer, device_id_type=MESH)

    loads = [
        pltpu.make_async_copy(load_ref.at[0, 0], edge.at[:, pl.ds(0, CASES)], in_sem.at[0]),
        pltpu.make_async_copy(schur_ref.at[0, 0], mat, in_sem.at[1]),
        pltpu.make_async_copy(len_ref.at[0], used, in_sem.at[2]),
        pltpu.make_async_copy(partner_ref.at[0, 0], rows_of, in_sem.at[3]),
        pltpu.make_async_copy(inv_ref, inv, in_sem.at[4]),
    ]
    rigid_loads = [
        pltpu.make_async_copy(rigid_ref.at[0, 0, :, d], edge.at[d, pl.ds(CASES, MODES)], in_sem.at[5 + d])
        for d in range(4)
    ]
    corner_loads = [
        pltpu.make_async_copy(
            schur_ref.at[0, 0, pl.ds(d * PAIR, PAIR), pl.ds(d * PAIR, PAIR)], corner.at[d], in_sem.at[9 + d]
        )
        for d in range(4)
    ]
    for copy in corner_loads + rigid_loads + loads[0:1] + loads[2:4] + loads[1:2] + loads[4:5]:
        copy.start()

    def send_all(src, dst_of, peers, stage):
        for i, peer in enumerate(peers):
            pltpu.make_async_remote_copy(
                src_ref=src, dst_ref=dst_of(i), send_sem=tree_send.at[stage], recv_sem=tree_recv.at[stage],
                device_id=peer, device_id_type=MESH,
            ).start()

    def whole(ref, stage, peer):
        return pltpu.make_async_remote_copy(
            src_ref=ref, dst_ref=ref, send_sem=tree_send.at[stage], recv_sem=tree_recv.at[stage],
            device_id=peer, device_id_type=MESH,
        )

    def halo_copies(src, dst, which):
        return [
            pltpu.make_async_remote_copy(
                src_ref=src.at[d], dst_ref=dst.at[d ^ 1], send_sem=halo_send.at[which, d],
                recv_sem=halo_recv.at[which, d ^ 1], device_id=near[d], device_id_type=MESH,
            )
            for d in range(4)
        ]

    pl.semaphore_wait(barrier, len(greeted))
    tell(0)
    tell(3)
    eye = iota((PAIR, PAIR), 0) == iota((PAIR, PAIR), 1)
    for d in range(4):
        corner_loads[d].wait()
        block = corner[d].astype(F32)
        diag = jnp.sum(jnp.where(eye, block, 0.0), axis=0, keepdims=True)
        edge[d, pl.ds(CASES + MODES, 2), :] = jnp.concatenate([diag, jnp.zeros((1, PAIR), F32)], axis=0)
    for copy in loads[0:1] + rigid_loads:
        copy.wait()
    edge_copies = halo_copies(edge, edge_in, 0)
    for copy in edge_copies:
        copy.start()
    hear(0)
    tell(1)
    hear(3)
    tell(4)

    for copy in loads[2:4]:
        copy.wait()
    lane = iota((1, PAIR), 1)
    live_parts = [(lane < jnp.broadcast_to(used[:, d : d + 1], (1, PAIR))).astype(F32) for d in range(4)]
    live = join(live_parts)
    sign_live = join([SIGNS[d] * live_parts[d] for d in range(4)])
    index = [rows_of[pl.ds(d, 1), :] for d in range(4)]

    def partner_rows(x, d):
        return jnp.take_along_axis(x, jnp.broadcast_to(index[d], x.shape), axis=1)

    coupling[...] = jnp.zeros((512, 512), F32)
    mode_row = iota((8, PAIR), 0) < MODES
    own = [edge[d] for d in range(4)]
    own_load = join([x[0:CASES] for x in own])
    own_rigid = join([jnp.where(mode_row, x[CASES:], 0.0) for x in own])
    own_diag = join([x[CASES + MODES : CASES + MODES + 1] for x in own])
    signed_rigid = sign_live * own_rigid

    hear(1)
    tell(2)
    hear(4)
    tell(5)
    for copy in edge_copies:
        copy.wait_recv()
    met = [partner_rows(edge_in[d], d) for d in range(4)]
    far_load = join([x[0:CASES] for x in met])
    far_rigid = [jnp.where(mode_row, x[CASES:], 0.0) for x in met]
    far_diag = join([x[CASES + MODES : CASES + MODES + 1] for x in met])
    weight = jnp.where(live > 0.0, 1.0 / (own_diag + far_diag), 0.0)
    nil = jnp.zeros((8, PAIR), F32)
    rhs = sign_live * (own_load - far_load)
    spread_own = sign_live * (own_rigid - join([far_rigid[0], far_rigid[1], nil, nil]))
    spread_low = -sign_live * join([nil, nil, far_rigid[2], nil])
    spread_high = -sign_live * join([nil, nil, nil, far_rigid[3]])
    basis = jnp.concatenate([spread_low, spread_own, spread_high], axis=0)

    weighted_rhs = weight * rhs
    first = jnp.concatenate([rhs, weighted_rhs, weight * basis, jnp.zeros((72, ROWS), F32)], axis=0)
    sums = nt(signed_rigid, first)
    row8 = iota((8, PAIR), 0)
    packed = sums + pltpu.roll(pltpu.roll(sums, 64, 1), 5, 0)
    out1[...] = packed[0:3]
    hear(2)
    send_all(out1, lambda i: z1_in.at[i, pl.ds(0, 3)], z_peers, 0)
    wide1 = sign_live * basis
    signed3 = jnp.concatenate(
        [part for k in range(3) for part in (wide1[8 * k : 8 * k + 8], weight * wide1[8 * k : 8 * k + 8])], axis=0
    )
    hear(5)
    tell(6)
    loads[1].wait()
    loads[4].wait()
    spread_row, spread_col = iota((512, 384), 0), iota((512, 384), 1)
    slot = spread_row & 7
    spread = jnp.where((slot < MODES) & ((spread_row >> 3) * MODES + slot == spread_col), 1.0, 0.0).astype(F32)
    padded[pl.ds(0, 8), :] = jnp.zeros((8, 512), F32)
    padded[pl.ds(520, 8), :] = jnp.zeros((8, 512), F32)
    padded[pl.ds(8, 512), :] = full_dot(full_dot(spread, inv[...], ((1,), (0,))), spread, ((1,), (1,)))
    inv3 = padded[pl.ds(pl.multiple_of(c * 8, 8), 24), :]
    padded_high[...], padded_low[...] = [part.astype(jnp.bfloat16) for part in split(padded[pl.ds(8, 512), :])]
    whole(z1_in.at[:, pl.ds(0, 3)], 0, z_peers[0]).wait_recv()
    total = out1[...]
    for i in range(NSUB - 1):
        total = total + z1_in[i, pl.ds(0, 3), :]
    g1[c, pl.ds(0, 3), :] = total
    hear(6)
    mine1 = g1.at[c, pl.ds(0, 3)]
    send_all(mine1, lambda i: mine1, clusters, 1)
    rest1 = g1.at[pl.ds(0, NCL - 1), pl.ds(0, 3)]
    whole(rest1, 1, clusters[0]).wait_recv()

    lane8 = iota((8, PAIR), 1)
    stacked = []
    for k in range(NCL):
        part = jnp.concatenate([g1[k, pl.ds(0, 3), :], jnp.zeros((5, PAIR), F32)], axis=0)
        part = part + pltpu.roll(pltpu.roll(part, 64, 1), 3, 0)
        stacked.append(part)
        column = 8 * (k - 1)
        moved = pltpu.roll(part, (column - 32) % PAIR, 1)
        tiles = sorted({(column + 8 * e) // PAIR for e in range(3) if 0 <= k - 1 + e < NCL})
        for t in tiles:
            first_lane = max(column, 0) - t * PAIR
            last_lane = min(column + 24, ROWS) - t * PAIR
            keep = (lane8 >= first_lane) & (lane8 < last_lane)
            coupling[pl.ds(8 * k, 8), pl.ds(t * PAIR, PAIR)] = jnp.where(keep, moved, 0.0)
    gathered = jnp.concatenate(stacked, axis=0)
    twice = nn(nn(inv3, coupling[...]), (padded_high[...], padded_low[...]))
    solver = jnp.concatenate([inv3, twice], axis=0)

    def solve(sums512):
        y = nn(solver, sums512)
        return join([y[0:24, 0:CASES], y[0:24, CASES : 2 * CASES] - y[24:48, 0:CASES]])

    def project(vector, coeffs):
        e = tn(coeffs, basis)
        projected = vector - e[0:CASES]
        return projected, weight * projected - e[CASES:]

    projected, direction = project(rhs, solve(gathered))
    ones = jnp.ones((8, ROWS), F32)
    operand = sign_live * direction
    image = jnp.dot(operand.astype(jnp.bfloat16), mat[...], preferred_element_type=F32)

    image_sums = nt(signed3, image)
    scalars = nt(ones, jnp.concatenate([0.5 * projected * direction, operand * image], axis=0))
    lanes2 = join([image_sums[8 * k : 8 * k + 8] for k in range(6)] + [scalars])
    out2[...] = lanes2[0:6]
    send_all(out2, lambda i: z2_in.at[i, pl.ds(0, 6)], z_peers, 3)
    for d in range(4):
        halo[d] = image[:, d * PAIR : (d + 1) * PAIR]
    image_copies = halo_copies(halo, halo_in, 1)
    for copy in image_copies:
        copy.start()
    whole(z2_in.at[:, pl.ds(0, 6)], 3, z_peers[0]).wait_recv()
    total = out2[...]
    for i in range(NSUB - 1):
        total = total + z2_in[i, pl.ds(0, 6), :]
    g2[c, pl.ds(0, 6), :] = total
    mine2 = g2.at[c, pl.ds(0, 6)]
    send_all(mine2, lambda i: mine2, clusters, 4)
    for copy in image_copies:
        copy.wait_recv()
    applied = sign_live * (image - join([partner_rows(halo_in[d], d) for d in range(4)]))
    rest2 = g2.at[pl.ds(0, NCL - 1), pl.ds(0, 6)]
    whole(rest2, 4, clusters[0]).wait_recv()

    parts = [
        jnp.concatenate([g2[k, pl.ds(0, 6), :], jnp.zeros((2, PAIR), F32)], axis=0) for k in range(NCL)
    ]
    shifted = []
    for k in range(NCL):
        x = pltpu.roll(parts[k], PAIR - 32, 1)
        if k + 1 < NCL:
            x = x + parts[k + 1]
        if k > 0:
            x = x + pltpu.roll(parts[k - 1], PAIR - 64, 1)
        shifted.append(x)
    sums_all = parts[0]
    for k in range(1, NCL):
        sums_all = sums_all + parts[k]

    def column(row, start, count):
        pick = jnp.where(iota((count * CASES, PAIR), 1) == iota((count * CASES, PAIR), 0) + start, 1.0, 0.0)
        return full_dot(pick.astype(F32), jnp.broadcast_to(row, (PAIR, PAIR)), ((1,), (1,)))

    both = column(sums_all[0:1], 96, 2)
    rho, curve = both[0:CASES], both[CASES:]
    step = tile4(rho / curve)
    projected_f, direction_f = project(applied, solve(jnp.concatenate(shifted, axis=0)))
    projected1 = projected - step * projected_f
    precond1 = direction - step * direction_f
    operand1 = sign_live * precond1
    high = operand1.astype(jnp.bfloat16)
    low = (operand1 - high.astype(F32)).astype(jnp.bfloat16)
    image2 = jnp.dot(jnp.concatenate([high, low], axis=0), mat[...], preferred_element_type=F32)
    image1 = image2[0:CASES] + image2[CASES:]

    scalars3 = nt(
        ones,
        jnp.concatenate(
            [
                0.5 * projected1 * precond1,
                operand1 * image1,
                operand1 * image + operand * image1,
                jnp.zeros((80, ROWS), F32),
            ],
            axis=0,
        ),
    )
    out3[...] = scalars3[0:1]
    send_all(out3, lambda i: z3_in.at[pl.ds(i, 1)], column_peers, 6)
    for d in range(4):
        halo2[d] = image1[:, d * PAIR : (d + 1) * PAIR]
    image_copies1 = halo_copies(halo2, halo2_in, 2)
    for copy in image_copies1:
        copy.start()
    def stage(which, *terms):
        for term, value in enumerate(terms):
            for d in range(4):
                staged[term, which, d] = value[:, d * PAIR : (d + 1) * PAIR]

    stage(0, step * direction, precond1, direction)
    whole(z3_in, 6, column_peers[0]).wait_recv()
    mid3[...] = out3[...] + jnp.sum(z3_in[...], axis=0, keepdims=True)
    send_all(mid3, lambda i: x3_in.at[pl.ds(i, 1)], plane, 7)
    for copy in image_copies1:
        copy.wait_recv()
    applied1 = sign_live * (image1 - join([partner_rows(halo2_in[d], d) for d in range(4)]))
    stage(1, rhs - step * applied, -applied1, -applied)
    write_out = pltpu.make_async_copy(staged, terms_ref, in_sem.at[0])
    write_out.start()
    whole(x3_in, 7, plane[0]).wait_recv()
    tail = column(mid3[...] + jnp.sum(x3_in[...], axis=0, keepdims=True), 0, 3)
    rho1, square, cross = tail[0:CASES], tail[CASES : 2 * CASES], tail[2 * CASES :]
    beta = rho1 / rho
    step1 = rho1 / (square + beta * cross + beta * beta * curve)
    step_ref[...] = step1
    older_ref[...] = step1 * beta
    write_out.wait()

    for copy in edge_copies + image_copies + image_copies1:
        copy.wait_send()
    whole(z1_in.at[:, pl.ds(0, 3)], 0, z_peers[0]).wait_send()
    whole(rest1, 1, clusters[0]).wait_send()
    whole(z2_in.at[:, pl.ds(0, 6)], 3, z_peers[0]).wait_send()
    whole(rest2, 4, clusters[0]).wait_send()
    whole(z3_in, 6, column_peers[0]).wait_send()
    whole(x3_in, 7, plane[0]).wait_send()


def shards(schur, load, rigid, lengths, partner, coarse_inverse):
    hbm = pl.BlockSpec(memory_space=pl.ANY)
    vmem = pl.BlockSpec(memory_space=pltpu.VMEM)
    terms_out = jax.ShapeDtypeStruct((3, 2) + load.shape[2:], F32)
    step_out = jax.ShapeDtypeStruct((CASES, PAIR), F32)
    terms, step, older = pl.pallas_call(
        kernel,
        out_shape=(terms_out, step_out, step_out),
        in_specs=[hbm] * 6,
        out_specs=(hbm, vmem, vmem),
        scratch_shapes=[
            pltpu.VMEM((3, 2, 4, CASES, PAIR), F32),
            pltpu.VMEM((ROWS, ROWS), jnp.bfloat16),
            pltpu.VMEM((4, PAIR, PAIR), jnp.bfloat16),
            pltpu.VMEM((384, 384), F32),
            pltpu.VMEM((1, 4), jnp.int32),
            pltpu.VMEM((4, PAIR), jnp.int32),
            pltpu.VMEM((528, 512), F32),
            pltpu.VMEM((512, 512), jnp.bfloat16),
            pltpu.VMEM((512, 512), jnp.bfloat16),
            pltpu.VMEM((512, 512), F32),
            pltpu.VMEM((4, 24, PAIR), F32),
            pltpu.VMEM((4, 24, PAIR), F32),
            pltpu.VMEM((4, CASES, PAIR), F32),
            pltpu.VMEM((4, CASES, PAIR), F32),
            pltpu.VMEM((4, CASES, PAIR), F32),
            pltpu.VMEM((4, CASES, PAIR), F32),
            pltpu.VMEM((3, PAIR), F32),
            pltpu.VMEM((NSUB - 1, 8, PAIR), F32),
            pltpu.VMEM((NCL, 8, PAIR), F32),
            pltpu.VMEM((6, PAIR), F32),
            pltpu.VMEM((NSUB - 1, 8, PAIR), F32),
            pltpu.VMEM((NCL, 8, PAIR), F32),
            pltpu.VMEM((1, PAIR), F32),
            pltpu.VMEM((2 * NSUB - 1, PAIR), F32),
            pltpu.VMEM((1, PAIR), F32),
            pltpu.VMEM((CHIPS - 1, PAIR), F32),
            pltpu.SemaphoreType.DMA((13,)),
            pltpu.SemaphoreType.DMA((3, 4)),
            pltpu.SemaphoreType.DMA((3, 4)),
            pltpu.SemaphoreType.DMA((9,)),
            pltpu.SemaphoreType.DMA((9,)),
            pltpu.SemaphoreType.REGULAR((7,)),
        ],
        compiler_params=pltpu.CompilerParams(
            collective_id=0, has_side_effects=True, vmem_limit_bytes=60 * 1024*1024
        ),
        name="feti",
    )(schur, load, jnp.transpose(rigid, (0, 1, 3, 2, 4)), lengths, partner, coarse_inverse)
    return tuple(
        (terms[0, k] + step[None] * terms[1, k] + older[None] * terms[2, k])[None, None] for k in range(2)
    )


def solution(mesh):
    in_specs = (
        P("clus", "sub", None, None),
        P("clus", "sub", None, None, None),
        P("clus", "sub", None, None, None),
        P("clus", "sub", None),
        P("clus", "sub", None, None),
        P(),
    )
    out_specs = (P("clus", "sub", None, None, None), P("clus", "sub", None, None, None))
    return jax.shard_map(shards, mesh=mesh, in_specs=in_specs, out_specs=out_specs, check_vma=False)
```

```python
import functools

import jax
import jax.numpy as jnp
from jax import lax
from jax.experimental import pallas as pl
from jax.experimental.pallas import tpu as pltpu
from jax.sharding import PartitionSpec as P

MESH = pl.DeviceIdType.MESH
HIGHEST = lax.Precision.HIGHEST
F32 = jnp.float32

NCL, NSUB, CHIPS = 64, 16, 32
CASES, MODES, PAIR = 16, 6, 128
ROWS = 4 * PAIR
SIGNS = (-1.0, 1.0, -1.0, 1.0)


def full_dot(a, b, dims):
    return lax.dot_general(a, b, (dims, ((), ())), precision=HIGHEST, preferred_element_type=F32)


def split(x):
    high = x.astype(jnp.bfloat16).astype(F32)
    return high, x - high


def dot3(a, b, dims):
    keep = 1 - dims[0][0]
    count = a.shape[keep]
    a_high, a_low = split(a)
    pair = jnp.concatenate([a_high, a_low], axis=keep).astype(jnp.bfloat16)
    b_high, b_low = b if isinstance(b, tuple) else [x.astype(jnp.bfloat16) for x in split(b)]

    def dot(x, y):
        return lax.dot_general(x, y, (dims, ((), ())), preferred_element_type=F32)

    both = dot(pair, b_high)
    return both[:count] + both[count:] + dot(a_high.astype(jnp.bfloat16), b_low)


def nn(a, b):
    return dot3(a, b, ((1,), (0,)))


def nt(a, b):
    return dot3(a, b, ((1,), (1,)))


def tn(a, b):
    return dot3(a, b, ((0,), (0,)))


def iota(shape, dim):
    return lax.broadcasted_iota(jnp.int32, shape, dim)


def join(parts):
    return jnp.concatenate(parts, axis=1)


def tile4(x):
    return join([x, x, x, x])


def kernel(
    schur_ref, load_ref, rigid_ref, len_ref, partner_ref, inv_ref, terms_ref, step_ref, older_ref, staged,
    mat, corner, inv, used, rows_of, padded, padded_high, padded_low, coupling, edge, edge_in, halo, halo_in, halo2, halo2_in,
    out1, z1_in, g1, out2, z2_in, g2, out3, z3_in, mid3, x3_in,
    in_sem, halo_send, halo_recv, tree_send, tree_recv, ready,
):
    c, s = lax.axis_index("clus"), lax.axis_index("sub")
    core, chip = lax.rem(c, 2), lax.div(c, 2)

    z_peers = [(c, lax.rem(s + o, NSUB)) for o in sorted(range(1, NSUB), key=lambda o: -min(o, NSUB - o))]
    y, x = lax.div(chip, 4), lax.rem(chip, 4)
    steps = sorted(range(1, CHIPS), key=lambda o: -(min(o // 4, 8 - o // 4) + min(o % 4, 4 - o % 4)))
    plane = [((lax.rem(y + o // 4, 8) * 4 + lax.rem(x + o % 4, 4)) * 2 + core, s) for o in steps]
    other = (chip * 2 + 1 - core, s)
    spans = sorted(
        range(1, NCL), key=lambda o: -(min(o // 8, 8 - o // 8) + min(o // 2 % 4, 4 - o // 2 % 4) + o % 2)
    )
    clusters = [
        ((lax.rem(y + o // 8, 8) * 4 + lax.rem(x + o // 2 % 4, 4)) * 2 + lax.rem(core + o % 2, 2), s) for o in spans
    ]
    columns = sorted(range(1, 2 * NSUB), key=lambda o: -(min(o // 2, NSUB - o // 2) + o % 2))
    column_peers = [(chip * 2 + lax.rem(core + o, 2), lax.rem(s + o // 2, NSUB)) for o in columns]
    near = [
        (c, lax.rem(s + NSUB - 1, NSUB)),
        (c, lax.rem(s + 1, NSUB)),
        (lax.rem(c + NCL - 1, NCL), s),
        (lax.rem(c + 1, NCL), s),
    ]
    away = (lax.rem(c + NCL - 1 + 2 * core, NCL), s)

    def z_by(o):
        return (c, lax.rem(s + o + NSUB, NSUB))

    def y_by(o):
        return ((lax.rem(y + o + 8, 8) * 4 + x) * 2 + core, s)

    def x_by(o):
        return ((y * 4 + lax.rem(x + o + 4, 4)) * 2 + core, s)

    greeted = [z_by(o * side) for o in (4, 3, 2, 1) for side in (-1, 1)] + [y_by(-1), y_by(1), x_by(-1), x_by(1), other, away]
    told = [
        [z_by(-4), z_by(4)],
        [x_by(-1), x_by(1)],
        [y_by(-1), y_by(1)],
        [y_by(-2), y_by(2)],
        [y_by(-1), y_by(1)],
    ]

    def tell(k):
        for peer in told[k]:
            pl.semaphore_signal(ready.at[k], inc=1, device_id=peer, device_id_type=MESH)

    def hear(k):
        pl.semaphore_wait(ready.at[k], 2)

    barrier = pltpu.get_barrier_semaphore()
    for peer in greeted:
        pl.semaphore_signal(barrier, inc=1, device_id=peer, device_id_type=MESH)

    loads = [
        pltpu.make_async_copy(load_ref.at[0, 0], edge.at[:, pl.ds(0, CASES)], in_sem.at[0]),
        pltpu.make_async_copy(schur_ref.at[0, 0], mat, in_sem.at[1]),
        pltpu.make_async_copy(len_ref.at[0], used, in_sem.at[2]),
        pltpu.make_async_copy(partner_ref.at[0, 0], rows_of, in_sem.at[3]),
        pltpu.make_async_copy(inv_ref, inv, in_sem.at[4]),
    ]
    rigid_loads = [
        pltpu.make_async_copy(rigid_ref.at[0, 0, :, d], edge.at[d, pl.ds(CASES, MODES)], in_sem.at[5 + d])
        for d in range(4)
    ]
    corner_loads = [
        pltpu.make_async_copy(
            schur_ref.at[0, 0, pl.ds(d * PAIR, PAIR), pl.ds(d * PAIR, PAIR)], corner.at[d], in_sem.at[9 + d]
        )
        for d in range(4)
    ]
    for copy in corner_loads + rigid_loads + loads[0:1] + loads[2:4] + loads[1:2] + loads[4:5]:
        copy.start()

    def send_all(src, dst_of, peers, stage):
        for i, peer in enumerate(peers):
            pltpu.make_async_remote_copy(
                src_ref=src, dst_ref=dst_of(i), send_sem=tree_send.at[stage], recv_sem=tree_recv.at[stage],
                device_id=peer, device_id_type=MESH,
            ).start()

    def whole(ref, stage, peer):
        return pltpu.make_async_remote_copy(
            src_ref=ref, dst_ref=ref, send_sem=tree_send.at[stage], recv_sem=tree_recv.at[stage],
            device_id=peer, device_id_type=MESH,
        )

    def halo_copies(src, dst, which):
        return [
            pltpu.make_async_remote_copy(
                src_ref=src.at[d], dst_ref=dst.at[d ^ 1], send_sem=halo_send.at[which, d],
                recv_sem=halo_recv.at[which, d ^ 1], device_id=near[d], device_id_type=MESH,
            )
            for d in range(4)
        ]

    pl.semaphore_wait(barrier, len(greeted))
    tell(0)
    tell(1)
    eye = iota((PAIR, PAIR), 0) == iota((PAIR, PAIR), 1)
    for d in range(4):
        corner_loads[d].wait()
        block = corner[d].astype(F32)
        diag = jnp.sum(jnp.where(eye, block, 0.0), axis=0, keepdims=True)
        edge[d, pl.ds(CASES + MODES, 2), :] = jnp.concatenate([diag, jnp.zeros((1, PAIR), F32)], axis=0)
    for copy in loads[0:1] + rigid_loads:
        copy.wait()
    edge_copies = halo_copies(edge, edge_in, 0)
    for copy in edge_copies:
        copy.start()
    hear(1)
    tell(2)

    for copy in loads[2:4]:
        copy.wait()
    lane = iota((1, PAIR), 1)
    live_parts = [(lane < jnp.broadcast_to(used[:, d : d + 1], (1, PAIR))).astype(F32) for d in range(4)]
    live = join(live_parts)
    sign_live = join([SIGNS[d] * live_parts[d] for d in range(4)])
    index = [rows_of[pl.ds(d, 1), :] for d in range(4)]

    def partner_rows(x, d):
        return jnp.take_along_axis(x, jnp.broadcast_to(index[d], x.shape), axis=1)

    coupling[...] = jnp.zeros((512, 512), F32)
    mode_row = iota((8, PAIR), 0) < MODES
    own = [edge[d] for d in range(4)]
    own_load = join([x[0:CASES] for x in own])
    own_rigid = join([jnp.where(mode_row, x[CASES:], 0.0) for x in own])
    own_diag = join([x[CASES + MODES : CASES + MODES + 1] for x in own])
    signed_rigid = sign_live * own_rigid

    hear(2)
    tell(3)
    for copy in edge_copies:
        copy.wait_recv()
    met = [partner_rows(edge_in[d], d) for d in range(4)]
    far_load = join([x[0:CASES] for x in met])
    far_rigid = [jnp.where(mode_row, x[CASES:], 0.0) for x in met]
    far_diag = join([x[CASES + MODES : CASES + MODES + 1] for x in met])
    weight = jnp.where(live > 0.0, 1.0 / (own_diag + far_diag), 0.0)
    nil = jnp.zeros((8, PAIR), F32)
    rhs = sign_live * (own_load - far_load)
    spread_own = sign_live * (own_rigid - join([far_rigid[0], far_rigid[1], nil, nil]))
    spread_low = -sign_live * join([nil, nil, far_rigid[2], nil])
    spread_high = -sign_live * join([nil, nil, nil, far_rigid[3]])
    basis = jnp.concatenate([spread_low, spread_own, spread_high], axis=0)

    weighted_rhs = weight * rhs
    first = jnp.concatenate([rhs, weighted_rhs, weight * basis, jnp.zeros((72, ROWS), F32)], axis=0)
    sums = nt(signed_rigid, first)
    row8 = iota((8, PAIR), 0)
    packed = sums + pltpu.roll(pltpu.roll(sums, 64, 1), 5, 0)
    out1[...] = packed[0:3]
    hear(0)
    send_all(out1, lambda i: z1_in.at[i, pl.ds(0, 3)], z_peers, 0)
    wide1 = sign_live * basis
    signed3 = jnp.concatenate(
        [part for k in range(3) for part in (wide1[8 * k : 8 * k + 8], weight * wide1[8 * k : 8 * k + 8])], axis=0
    )
    hear(3)
    tell(4)
    loads[1].wait()
    loads[4].wait()
    spread_row, spread_col = iota((512, 384), 0), iota((512, 384), 1)
    slot = spread_row & 7
    spread = jnp.where((slot < MODES) & ((spread_row >> 3) * MODES + slot == spread_col), 1.0, 0.0).astype(F32)
    padded[pl.ds(0, 8), :] = jnp.zeros((8, 512), F32)
    padded[pl.ds(520, 8), :] = jnp.zeros((8, 512), F32)
    padded[pl.ds(8, 512), :] = full_dot(full_dot(spread, inv[...], ((1,), (0,))), spread, ((1,), (1,)))
    inv3 = padded[pl.ds(pl.multiple_of(c * 8, 8), 24), :]
    padded_high[...], padded_low[...] = [part.astype(jnp.bfloat16) for part in split(padded[pl.ds(8, 512), :])]
    whole(z1_in.at[:, pl.ds(0, 3)], 0, z_peers[0]).wait_recv()
    total = out1[...]
    for i in range(NSUB - 1):
        total = total + z1_in[i, pl.ds(0, 3), :]
    g1[c, pl.ds(0, 3), :] = total
    hear(4)
    mine1 = g1.at[c, pl.ds(0, 3)]
    send_all(mine1, lambda i: mine1, clusters, 1)
    rest1 = g1.at[pl.ds(0, NCL - 1), pl.ds(0, 3)]
    whole(rest1, 1, clusters[0]).wait_recv()

    lane8 = iota((8, PAIR), 1)
    stacked = []
    for k in range(NCL):
        part = jnp.concatenate([g1[k, pl.ds(0, 3), :], jnp.zeros((5, PAIR), F32)], axis=0)
        part = part + pltpu.roll(pltpu.roll(part, 64, 1), 3, 0)
        stacked.append(part)
        column = 8 * (k - 1)
        moved = pltpu.roll(part, (column - 32) % PAIR, 1)
        tiles = sorted({(column + 8 * e) // PAIR for e in range(3) if 0 <= k - 1 + e < NCL})
        for t in tiles:
            first_lane = max(column, 0) - t * PAIR
            last_lane = min(column + 24, ROWS) - t * PAIR
            keep = (lane8 >= first_lane) & (lane8 < last_lane)
            coupling[pl.ds(8 * k, 8), pl.ds(t * PAIR, PAIR)] = jnp.where(keep, moved, 0.0)
    gathered = jnp.concatenate(stacked, axis=0)
    twice = nn(nn(inv3, coupling[...]), (padded_high[...], padded_low[...]))
    solver = jnp.concatenate([inv3, twice], axis=0)

    def solve(sums512):
        y = nn(solver, sums512)
        return join([y[0:24, 0:CASES], y[0:24, CASES : 2 * CASES] - y[24:48, 0:CASES]])

    def project(vector, coeffs):
        e = tn(coeffs, basis)
        projected = vector - e[0:CASES]
        return projected, weight * projected - e[CASES:]

    projected, direction = project(rhs, solve(gathered))
    ones = jnp.ones((8, ROWS), F32)
    operand = sign_live * direction
    image = jnp.dot(operand.astype(jnp.bfloat16), mat[...], preferred_element_type=F32)

    image_sums = nt(signed3, image)
    scalars = nt(ones, jnp.concatenate([0.5 * projected * direction, operand * image], axis=0))
    lanes2 = join([image_sums[8 * k : 8 * k + 8] for k in range(6)] + [scalars])
    lane8, sixth = iota((8, PAIR), 1), jnp.broadcast_to(lanes2[5:6], (8, PAIR))
    for row in range(3):
        here = (row8 == row) & (lane8 >= 96)
        lanes2 = jnp.where(here, pltpu.roll(sixth, 96 - 32 * row, 1), lanes2)
    out2[...] = lanes2[0:5]
    send_all(out2, lambda i: z2_in.at[i, pl.ds(0, 5)], z_peers, 3)
    for d in range(4):
        halo[d] = image[:, d * PAIR : (d + 1) * PAIR]
    image_copies = halo_copies(halo, halo_in, 1)
    for copy in image_copies:
        copy.start()
    whole(z2_in.at[:, pl.ds(0, 5)], 3, z_peers[0]).wait_recv()
    total = out2[...]
    for i in range(NSUB - 1):
        total = total + z2_in[i, pl.ds(0, 5), :]
    g2[c, pl.ds(0, 5), :] = total
    mine2 = g2.at[c, pl.ds(0, 5)]
    send_all(mine2, lambda i: mine2, clusters, 4)
    for copy in image_copies:
        copy.wait_recv()
    applied = sign_live * (image - join([partner_rows(halo_in[d], d) for d in range(4)]))
    rest2 = g2.at[pl.ds(0, NCL - 1), pl.ds(0, 5)]
    whole(rest2, 4, clusters[0]).wait_recv()

    parts = [
        jnp.concatenate([g2[k, pl.ds(0, 5), :], jnp.zeros((3, PAIR), F32)], axis=0) for k in range(NCL)
    ]
    shifted = []
    last_mode = (row8 == 5) & (lane8 < 32)
    for k in range(NCL):
        last = jnp.broadcast_to(g2[k, pl.ds(1, 1), :], (8, PAIR))
        if k + 1 < NCL:
            last = last + jnp.broadcast_to(g2[k + 1, pl.ds(0, 1), :], (8, PAIR))
        if k > 0:
            last = last + jnp.broadcast_to(g2[k - 1, pl.ds(2, 1), :], (8, PAIR))
        x = pltpu.roll(parts[k], PAIR - 32, 1)
        if k + 1 < NCL:
            x = x + parts[k + 1]
        if k > 0:
            x = x + pltpu.roll(parts[k - 1], PAIR - 64, 1)
        shifted.append(jnp.where(last_mode, pltpu.roll(last, 32, 1), x))
    sums_all = parts[0]
    for k in range(1, NCL):
        sums_all = sums_all + parts[k]

    def column(row, start, count):
        pick = jnp.where(iota((count * CASES, PAIR), 1) == iota((count * CASES, PAIR), 0) + start, 1.0, 0.0)
        return full_dot(pick.astype(F32), jnp.broadcast_to(row, (PAIR, PAIR)), ((1,), (1,)))

    both = column(sums_all[3:4], 96, 2)
    rho, curve = both[0:CASES], both[CASES:]
    step = tile4(rho / curve)
    projected_f, direction_f = project(applied, solve(jnp.concatenate(shifted, axis=0)))
    projected1 = projected - step * projected_f
    precond1 = direction - step * direction_f
    operand1 = sign_live * precond1
    high = operand1.astype(jnp.bfloat16)
    low = (operand1 - high.astype(F32)).astype(jnp.bfloat16)
    image2 = jnp.dot(jnp.concatenate([high, low], axis=0), mat[...], preferred_element_type=F32)
    image1 = image2[0:CASES] + image2[CASES:]

    scalars3 = nt(
        ones,
        jnp.concatenate(
            [
                0.5 * projected1 * precond1,
                operand1 * image1,
                operand1 * image + operand * image1,
                jnp.zeros((80, ROWS), F32),
            ],
            axis=0,
        ),
    )
    out3[...] = scalars3[0:1]
    send_all(out3, lambda i: z3_in.at[pl.ds(i, 1)], column_peers, 6)
    for d in range(4):
        halo2[d] = image1[:, d * PAIR : (d + 1) * PAIR]
    image_copies1 = halo_copies(halo2, halo2_in, 2)
    for copy in image_copies1:
        copy.start()
    def stage(which, *terms):
        for term, value in enumerate(terms):
            for d in range(4):
                staged[term, which, d] = value[:, d * PAIR : (d + 1) * PAIR]

    stage(0, step * direction, precond1, direction)
    whole(z3_in, 6, column_peers[0]).wait_recv()
    mid3[...] = out3[...] + jnp.sum(z3_in[...], axis=0, keepdims=True)
    send_all(mid3, lambda i: x3_in.at[pl.ds(i, 1)], plane, 7)
    for copy in image_copies1:
        copy.wait_recv()
    applied1 = sign_live * (image1 - join([partner_rows(halo2_in[d], d) for d in range(4)]))
    stage(1, rhs - step * applied, -applied1, -applied)
    write_out = pltpu.make_async_copy(staged, terms_ref, in_sem.at[0])
    write_out.start()
    whole(x3_in, 7, plane[0]).wait_recv()
    tail = column(mid3[...] + jnp.sum(x3_in[...], axis=0, keepdims=True), 0, 3)
    rho1, square, cross = tail[0:CASES], tail[CASES : 2 * CASES], tail[2 * CASES :]
    beta = rho1 / rho
    step1 = rho1 / (square + beta * cross + beta * beta * curve)
    step_ref[...] = step1
    older_ref[...] = step1 * beta
    write_out.wait()

    for copy in edge_copies + image_copies + image_copies1:
        copy.wait_send()
    whole(z1_in.at[:, pl.ds(0, 3)], 0, z_peers[0]).wait_send()
    whole(rest1, 1, clusters[0]).wait_send()
    whole(z2_in.at[:, pl.ds(0, 5)], 3, z_peers[0]).wait_send()
    whole(rest2, 4, clusters[0]).wait_send()
    whole(z3_in, 6, column_peers[0]).wait_send()
    whole(x3_in, 7, plane[0]).wait_send()


def shards(schur, load, rigid, lengths, partner, coarse_inverse):
    hbm = pl.BlockSpec(memory_space=pl.ANY)
    vmem = pl.BlockSpec(memory_space=pltpu.VMEM)
    terms_out = jax.ShapeDtypeStruct((3, 2) + load.shape[2:], F32)
    step_out = jax.ShapeDtypeStruct((CASES, PAIR), F32)
    terms, step, older = pl.pallas_call(
        kernel,
        out_shape=(terms_out, step_out, step_out),
        in_specs=[hbm] * 6,
        out_specs=(hbm, vmem, vmem),
        scratch_shapes=[
            pltpu.VMEM((3, 2, 4, CASES, PAIR), F32),
            pltpu.VMEM((ROWS, ROWS), jnp.bfloat16),
            pltpu.VMEM((4, PAIR, PAIR), jnp.bfloat16),
            pltpu.VMEM((384, 384), F32),
            pltpu.VMEM((1, 4), jnp.int32),
            pltpu.VMEM((4, PAIR), jnp.int32),
            pltpu.VMEM((528, 512), F32),
            pltpu.VMEM((512, 512), jnp.bfloat16),
            pltpu.VMEM((512, 512), jnp.bfloat16),
            pltpu.VMEM((512, 512), F32),
            pltpu.VMEM((4, 24, PAIR), F32),
            pltpu.VMEM((4, 24, PAIR), F32),
            pltpu.VMEM((4, CASES, PAIR), F32),
            pltpu.VMEM((4, CASES, PAIR), F32),
            pltpu.VMEM((4, CASES, PAIR), F32),
            pltpu.VMEM((4, CASES, PAIR), F32),
            pltpu.VMEM((3, PAIR), F32),
            pltpu.VMEM((NSUB - 1, 8, PAIR), F32),
            pltpu.VMEM((NCL, 8, PAIR), F32),
            pltpu.VMEM((5, PAIR), F32),
            pltpu.VMEM((NSUB - 1, 8, PAIR), F32),
            pltpu.VMEM((NCL, 8, PAIR), F32),
            pltpu.VMEM((1, PAIR), F32),
            pltpu.VMEM((2 * NSUB - 1, PAIR), F32),
            pltpu.VMEM((1, PAIR), F32),
            pltpu.VMEM((CHIPS - 1, PAIR), F32),
            pltpu.SemaphoreType.DMA((13,)),
            pltpu.SemaphoreType.DMA((3, 4)),
            pltpu.SemaphoreType.DMA((3, 4)),
            pltpu.SemaphoreType.DMA((9,)),
            pltpu.SemaphoreType.DMA((9,)),
            pltpu.SemaphoreType.REGULAR((5,)),
        ],
        compiler_params=pltpu.CompilerParams(
            collective_id=0, has_side_effects=True, vmem_limit_bytes=60 * 1024*1024
        ),
        name="feti",
    )(schur, load, jnp.transpose(rigid, (0, 1, 3, 2, 4)), lengths, partner, coarse_inverse)
    return tuple(
        (terms[0, k] + step[None] * terms[1, k] + older[None] * terms[2, k])[None, None] for k in range(2)
    )


def solution(mesh):
    in_specs = (
        P("clus", "sub", None, None),
        P("clus", "sub", None, None, None),
        P("clus", "sub", None, None, None),
        P("clus", "sub", None),
        P("clus", "sub", None, None),
        P(),
    )
    out_specs = (P("clus", "sub", None, None, None), P("clus", "sub", None, None, None))
    return jax.shard_map(shards, mesh=mesh, in_specs=in_specs, out_specs=out_specs, check_vma=False)
```

```python
import functools

import jax
import jax.numpy as jnp
from jax import lax
from jax.experimental import pallas as pl
from jax.experimental.pallas import tpu as pltpu
from jax.sharding import PartitionSpec as P

MESH = pl.DeviceIdType.MESH
HIGHEST = lax.Precision.HIGHEST
F32 = jnp.float32

NCL, NSUB, CHIPS = 64, 16, 32
CASES, MODES, PAIR = 16, 6, 128
ROWS = 4 * PAIR
SIGNS = (-1.0, 1.0, -1.0, 1.0)


def full_dot(a, b, dims):
    return lax.dot_general(a, b, (dims, ((), ())), precision=HIGHEST, preferred_element_type=F32)


def split(x):
    high = x.astype(jnp.bfloat16).astype(F32)
    return high, x - high


def dot3(a, b, dims):
    keep = 1 - dims[0][0]
    count = a.shape[keep]
    a_high, a_low = split(a)
    pair = jnp.concatenate([a_high, a_low], axis=keep).astype(jnp.bfloat16)
    b_high, b_low = b if isinstance(b, tuple) else [x.astype(jnp.bfloat16) for x in split(b)]

    def dot(x, y):
        return lax.dot_general(x, y, (dims, ((), ())), preferred_element_type=F32)

    both = dot(pair, b_high)
    return both[:count] + both[count:] + dot(a_high.astype(jnp.bfloat16), b_low)


def nn(a, b):
    return dot3(a, b, ((1,), (0,)))


def nt(a, b):
    return dot3(a, b, ((1,), (1,)))


def tn(a, b):
    return dot3(a, b, ((0,), (0,)))


def iota(shape, dim):
    return lax.broadcasted_iota(jnp.int32, shape, dim)


def join(parts):
    return jnp.concatenate(parts, axis=1)


def tile4(x):
    return join([x, x, x, x])


def kernel(
    schur_ref, load_ref, rigid_ref, len_ref, partner_ref, inv_ref, terms_ref, step_ref, older_ref, staged,
    mat, corner, inv, used, rows_of, padded, padded_high, padded_low, coupling, edge, edge_in, halo, halo_in, halo2, halo2_in,
    out1, z1_in, g1, out2, z2_in, g2, out3, z3_in, mid3, x3_in,
    in_sem, halo_send, halo_recv, tree_send, tree_recv, ready,
):
    c, s = lax.axis_index("clus"), lax.axis_index("sub")
    core, chip = lax.rem(c, 2), lax.div(c, 2)

    z_peers = [(c, lax.rem(s + o, NSUB)) for o in sorted(range(1, NSUB), key=lambda o: -min(o, NSUB - o))]
    y, x = lax.div(chip, 4), lax.rem(chip, 4)
    steps = sorted(range(1, CHIPS), key=lambda o: -(min(o // 4, 8 - o // 4) + min(o % 4, 4 - o % 4)))
    plane = [((lax.rem(y + o // 4, 8) * 4 + lax.rem(x + o % 4, 4)) * 2 + core, s) for o in steps]
    other = (chip * 2 + 1 - core, s)
    spans = sorted(
        range(1, NCL), key=lambda o: -(min(o // 8, 8 - o // 8) + min(o // 2 % 4, 4 - o // 2 % 4) + o % 2)
    )
    clusters = [
        ((lax.rem(y + o // 8, 8) * 4 + lax.rem(x + o // 2 % 4, 4)) * 2 + lax.rem(core + o % 2, 2), s) for o in spans
    ]
    columns = sorted(range(1, 2 * NSUB), key=lambda o: -(min(o // 2, NSUB - o // 2) + o % 2))
    column_peers = [(chip * 2 + lax.rem(core + o, 2), lax.rem(s + o // 2, NSUB)) for o in columns]
    near = [
        (c, lax.rem(s + NSUB - 1, NSUB)),
        (c, lax.rem(s + 1, NSUB)),
        (lax.rem(c + NCL - 1, NCL), s),
        (lax.rem(c + 1, NCL), s),
    ]
    away = (lax.rem(c + NCL - 1 + 2 * core, NCL), s)

    def z_by(o):
        return (c, lax.rem(s + o + NSUB, NSUB))

    def y_by(o):
        return ((lax.rem(y + o + 8, 8) * 4 + x) * 2 + core, s)

    def x_by(o):
        return ((y * 4 + lax.rem(x + o + 4, 4)) * 2 + core, s)

    greeted = [z_by(o * side) for o in (4, 3, 2, 1) for side in (-1, 1)] + [y_by(-1), y_by(1), x_by(-1), x_by(1), other, away]
    told = [
        [z_by(-4), z_by(4)],
        [x_by(-1), x_by(1)],
        [y_by(-1), y_by(1)],
        [y_by(-2), y_by(2)],
        [y_by(-1), y_by(1)],
    ]

    def tell(k):
        for peer in told[k]:
            pl.semaphore_signal(ready.at[k], inc=1, device_id=peer, device_id_type=MESH)

    def hear(k):
        pl.semaphore_wait(ready.at[k], 2)

    barrier = pltpu.get_barrier_semaphore()
    for peer in greeted:
        pl.semaphore_signal(barrier, inc=1, device_id=peer, device_id_type=MESH)

    loads = [
        pltpu.make_async_copy(load_ref.at[0, 0], edge.at[:, pl.ds(0, CASES)], in_sem.at[0]),
        pltpu.make_async_copy(schur_ref.at[0, 0], mat, in_sem.at[1]),
        pltpu.make_async_copy(len_ref.at[0], used, in_sem.at[2]),
        pltpu.make_async_copy(partner_ref.at[0, 0], rows_of, in_sem.at[3]),
        pltpu.make_async_copy(inv_ref, inv, in_sem.at[4]),
    ]
    rigid_loads = [
        pltpu.make_async_copy(rigid_ref.at[0, 0, :, d], edge.at[d, pl.ds(CASES, MODES)], in_sem.at[5 + d])
        for d in range(4)
    ]
    corner_loads = [
        pltpu.make_async_copy(
            schur_ref.at[0, 0, pl.ds(d * PAIR, PAIR), pl.ds(d * PAIR, PAIR)], corner.at[d], in_sem.at[9 + d]
        )
        for d in range(4)
    ]
    for copy in corner_loads + rigid_loads + loads[0:1] + loads[2:4] + loads[1:2] + loads[4:5]:
        copy.start()

    def send_all(src, dst_of, peers, stage):
        for i, peer in enumerate(peers):
            pltpu.make_async_remote_copy(
                src_ref=src, dst_ref=dst_of(i), send_sem=tree_send.at[stage], recv_sem=tree_recv.at[stage],
                device_id=peer, device_id_type=MESH,
            ).start()

    def whole(ref, stage, peer):
        return pltpu.make_async_remote_copy(
            src_ref=ref, dst_ref=ref, send_sem=tree_send.at[stage], recv_sem=tree_recv.at[stage],
            device_id=peer, device_id_type=MESH,
        )

    def halo_copies(src, dst, which):
        return [
            pltpu.make_async_remote_copy(
                src_ref=src.at[d], dst_ref=dst.at[d ^ 1], send_sem=halo_send.at[which, d],
                recv_sem=halo_recv.at[which, d ^ 1], device_id=near[d], device_id_type=MESH,
            )
            for d in range(4)
        ]

    pl.semaphore_wait(barrier, len(greeted))
    tell(0)
    tell(1)
    eye = iota((PAIR, PAIR), 0) == iota((PAIR, PAIR), 1)
    for d in range(4):
        corner_loads[d].wait()
        block = corner[d].astype(F32)
        diag = jnp.sum(jnp.where(eye, block, 0.0), axis=0, keepdims=True)
        edge[d, pl.ds(CASES + MODES, 2), :] = jnp.concatenate([diag, jnp.zeros((1, PAIR), F32)], axis=0)
    for copy in loads[0:1] + rigid_loads:
        copy.wait()
    edge_copies = halo_copies(edge, edge_in, 0)
    for copy in edge_copies:
        copy.start()
    hear(1)
    tell(2)

    for copy in loads[2:4]:
        copy.wait()
    lane = iota((1, PAIR), 1)
    live_parts = [(lane < jnp.broadcast_to(used[:, d : d + 1], (1, PAIR))).astype(F32) for d in range(4)]
    live = join(live_parts)
    sign_live = join([SIGNS[d] * live_parts[d] for d in range(4)])
    index = [rows_of[pl.ds(d, 1), :] for d in range(4)]

    def partner_rows(x, d):
        return jnp.take_along_axis(x, jnp.broadcast_to(index[d], x.shape), axis=1)

    coupling[...] = jnp.zeros((512, 512), F32)
    mode_row = iota((8, PAIR), 0) < MODES
    own = [edge[d] for d in range(4)]
    own_load = join([x[0:CASES] for x in own])
    own_rigid = join([jnp.where(mode_row, x[CASES:], 0.0) for x in own])
    own_diag = join([x[CASES + MODES : CASES + MODES + 1] for x in own])
    signed_rigid = sign_live * own_rigid

    hear(2)
    tell(3)
    for copy in edge_copies:
        copy.wait_recv()
    met = [partner_rows(edge_in[d], d) for d in range(4)]
    far_load = join([x[0:CASES] for x in met])
    far_rigid = [jnp.where(mode_row, x[CASES:], 0.0) for x in met]
    far_diag = join([x[CASES + MODES : CASES + MODES + 1] for x in met])
    weight = jnp.where(live > 0.0, 1.0 / (own_diag + far_diag), 0.0)
    nil = jnp.zeros((8, PAIR), F32)
    rhs = sign_live * (own_load - far_load)
    spread_own = sign_live * (own_rigid - join([far_rigid[0], far_rigid[1], nil, nil]))
    spread_low = -sign_live * join([nil, nil, far_rigid[2], nil])
    spread_high = -sign_live * join([nil, nil, nil, far_rigid[3]])
    basis = jnp.concatenate([spread_low, spread_own, spread_high], axis=0)

    weighted_rhs = weight * rhs
    first = jnp.concatenate([rhs, weighted_rhs, weight * basis, jnp.zeros((72, ROWS), F32)], axis=0)
    sums = nt(signed_rigid, first)
    row8 = iota((8, PAIR), 0)
    packed = sums + pltpu.roll(pltpu.roll(sums, 64, 1), 5, 0)
    out1[...] = packed[0:3]
    hear(0)
    send_all(out1, lambda i: z1_in.at[i, pl.ds(0, 3)], z_peers, 0)
    wide1 = sign_live * basis
    signed3 = jnp.concatenate(
        [part for k in range(3) for part in (wide1[8 * k : 8 * k + 8], weight * wide1[8 * k : 8 * k + 8])], axis=0
    )
    hear(3)
    tell(4)
    loads[1].wait()
    loads[4].wait()
    spread_row, spread_col = iota((512, 384), 0), iota((512, 384), 1)
    slot = spread_row & 7
    spread = jnp.where((slot < MODES) & ((spread_row >> 3) * MODES + slot == spread_col), 1.0, 0.0).astype(F32)
    padded[pl.ds(0, 8), :] = jnp.zeros((8, 512), F32)
    padded[pl.ds(520, 8), :] = jnp.zeros((8, 512), F32)
    padded[pl.ds(8, 512), :] = full_dot(full_dot(spread, inv[...], ((1,), (0,))), spread, ((1,), (1,)))
    inv3 = padded[pl.ds(pl.multiple_of(c * 8, 8), 24), :]
    padded_high[...], padded_low[...] = [part.astype(jnp.bfloat16) for part in split(padded[pl.ds(8, 512), :])]
    whole(z1_in.at[:, pl.ds(0, 3)], 0, z_peers[0]).wait_recv()
    total = out1[...]
    for i in range(NSUB - 1):
        total = total + z1_in[i, pl.ds(0, 3), :]
    g1[c, pl.ds(0, 3), :] = total
    hear(4)
    mine1 = g1.at[c, pl.ds(0, 3)]
    send_all(mine1, lambda i: mine1, clusters, 1)
    rest1 = g1.at[pl.ds(0, NCL - 1), pl.ds(0, 3)]
    whole(rest1, 1, clusters[0]).wait_recv()

    lane8 = iota((8, PAIR), 1)
    stacked = []
    for k in range(NCL):
        part = jnp.concatenate([g1[k, pl.ds(0, 3), :], jnp.zeros((5, PAIR), F32)], axis=0)
        part = part + pltpu.roll(pltpu.roll(part, 64, 1), 3, 0)
        stacked.append(part)
        column = 8 * (k - 1)
        moved = pltpu.roll(part, (column - 32) % PAIR, 1)
        tiles = sorted({(column + 8 * e) // PAIR for e in range(3) if 0 <= k - 1 + e < NCL})
        for t in tiles:
            first_lane = max(column, 0) - t * PAIR
            last_lane = min(column + 24, ROWS) - t * PAIR
            keep = (lane8 >= first_lane) & (lane8 < last_lane)
            coupling[pl.ds(8 * k, 8), pl.ds(t * PAIR, PAIR)] = jnp.where(keep, moved, 0.0)
    gathered = jnp.concatenate(stacked, axis=0)
    twice = nn(nn(inv3, coupling[...]), (padded_high[...], padded_low[...]))
    solver = jnp.concatenate([inv3, twice], axis=0)

    def solve(sums512):
        y = nn(solver, sums512)
        return join([y[0:24, 0:CASES], y[0:24, CASES : 2 * CASES] - y[24:48, 0:CASES]])

    def project(vector, coeffs):
        e = tn(coeffs, basis)
        projected = vector - e[0:CASES]
        return projected, weight * projected - e[CASES:]

    projected, direction = project(rhs, solve(gathered))
    ones = jnp.ones((8, ROWS), F32)
    operand = sign_live * direction
    image = jnp.dot(operand.astype(jnp.bfloat16), mat[...], preferred_element_type=F32)

    image_sums = nt(signed3, image)
    scalars = nt(ones, jnp.concatenate([0.5 * projected * direction, operand * image], axis=0))
    lanes2 = join([image_sums[8 * k : 8 * k + 8] for k in range(6)] + [scalars])
    lane8, sixth = iota((8, PAIR), 1), jnp.broadcast_to(lanes2[5:6], (8, PAIR))
    for row in range(3):
        here = (row8 == row) & (lane8 >= 96)
        lanes2 = jnp.where(here, pltpu.roll(sixth, 96 - 32 * row, 1), lanes2)
    out2[...] = lanes2[0:5]
    send_all(out2, lambda i: z2_in.at[i, pl.ds(0, 5)], z_peers, 3)
    for d in range(4):
        halo[d] = image[:, d * PAIR : (d + 1) * PAIR]
    image_copies = halo_copies(halo, halo_in, 1)
    for copy in image_copies:
        copy.start()
    whole(z2_in.at[:, pl.ds(0, 5)], 3, z_peers[0]).wait_recv()
    total = out2[...]
    for i in range(NSUB - 1):
        total = total + z2_in[i, pl.ds(0, 5), :]
    g2[c, pl.ds(0, 5), :] = total
    mine2 = g2.at[c, pl.ds(0, 5)]
    send_all(mine2, lambda i: mine2, clusters, 4)
    for copy in image_copies:
        copy.wait_recv()
    applied = sign_live * (image - join([partner_rows(halo_in[d], d) for d in range(4)]))
    rest2 = g2.at[pl.ds(0, NCL - 1), pl.ds(0, 5)]
    whole(rest2, 4, clusters[0]).wait_recv()

    parts = [
        jnp.concatenate([g2[k, pl.ds(0, 5), :], jnp.zeros((3, PAIR), F32)], axis=0) for k in range(NCL)
    ]
    shifted = []
    last_mode = (row8 == 5) & (lane8 < 32)
    for k in range(NCL):
        last = jnp.broadcast_to(g2[k, pl.ds(1, 1), :], (8, PAIR))
        if k + 1 < NCL:
            last = last + jnp.broadcast_to(g2[k + 1, pl.ds(0, 1), :], (8, PAIR))
        if k > 0:
            last = last + jnp.broadcast_to(g2[k - 1, pl.ds(2, 1), :], (8, PAIR))
        x = pltpu.roll(parts[k], PAIR - 32, 1)
        if k + 1 < NCL:
            x = x + parts[k + 1]
        if k > 0:
            x = x + pltpu.roll(parts[k - 1], PAIR - 64, 1)
        shifted.append(jnp.where(last_mode, pltpu.roll(last, 32, 1), x))
    sums_all = parts[0]
    for k in range(1, NCL):
        sums_all = sums_all + parts[k]

    def column(row, start, count):
        pick = jnp.where(iota((count * CASES, PAIR), 1) == iota((count * CASES, PAIR), 0) + start, 1.0, 0.0)
        return nt(pick.astype(F32), jnp.broadcast_to(row, (PAIR, PAIR)))

    both = column(sums_all[3:4], 96, 2)
    rho, curve = both[0:CASES], both[CASES:]
    step = tile4(rho / curve)
    projected_f, direction_f = project(applied, solve(jnp.concatenate(shifted, axis=0)))
    projected1 = projected - step * projected_f
    precond1 = direction - step * direction_f
    operand1 = sign_live * precond1
    high = operand1.astype(jnp.bfloat16)
    low = (operand1 - high.astype(F32)).astype(jnp.bfloat16)
    image2 = jnp.dot(jnp.concatenate([high, low], axis=0), mat[...], preferred_element_type=F32)
    image1 = image2[0:CASES] + image2[CASES:]

    scalars3 = nt(
        ones,
        jnp.concatenate(
            [
                0.5 * projected1 * precond1,
                operand1 * image1,
                operand1 * image + operand * image1,
                jnp.zeros((80, ROWS), F32),
            ],
            axis=0,
        ),
    )
    out3[...] = scalars3[0:1]
    send_all(out3, lambda i: z3_in.at[pl.ds(i, 1)], column_peers, 6)
    for d in range(4):
        halo2[d] = image1[:, d * PAIR : (d + 1) * PAIR]
    image_copies1 = halo_copies(halo2, halo2_in, 2)
    for copy in image_copies1:
        copy.start()
    def stage(which, *terms):
        for term, value in enumerate(terms):
            for d in range(4):
                staged[term, which, d] = value[:, d * PAIR : (d + 1) * PAIR]

    stage(0, step * direction, precond1, direction)
    whole(z3_in, 6, column_peers[0]).wait_recv()
    mid3[...] = out3[...] + jnp.sum(z3_in[...], axis=0, keepdims=True)
    send_all(mid3, lambda i: x3_in.at[pl.ds(i, 1)], plane, 7)
    for copy in image_copies1:
        copy.wait_recv()
    applied1 = sign_live * (image1 - join([partner_rows(halo2_in[d], d) for d in range(4)]))
    stage(1, rhs - step * applied, -applied1, -applied)
    write_out = pltpu.make_async_copy(staged, terms_ref, in_sem.at[0])
    write_out.start()
    whole(x3_in, 7, plane[0]).wait_recv()
    tail = column(mid3[...] + jnp.sum(x3_in[...], axis=0, keepdims=True), 0, 3)
    rho1, square, cross = tail[0:CASES], tail[CASES : 2 * CASES], tail[2 * CASES :]
    beta = rho1 / rho
    step1 = rho1 / (square + beta * cross + beta * beta * curve)
    step_ref[...] = step1
    older_ref[...] = step1 * beta
    write_out.wait()

    for copy in edge_copies + image_copies + image_copies1:
        copy.wait_send()
    whole(z1_in.at[:, pl.ds(0, 3)], 0, z_peers[0]).wait_send()
    whole(rest1, 1, clusters[0]).wait_send()
    whole(z2_in.at[:, pl.ds(0, 5)], 3, z_peers[0]).wait_send()
    whole(rest2, 4, clusters[0]).wait_send()
    whole(z3_in, 6, column_peers[0]).wait_send()
    whole(x3_in, 7, plane[0]).wait_send()


def shards(schur, load, rigid, lengths, partner, coarse_inverse):
    hbm = pl.BlockSpec(memory_space=pl.ANY)
    vmem = pl.BlockSpec(memory_space=pltpu.VMEM)
    terms_out = jax.ShapeDtypeStruct((3, 2) + load.shape[2:], F32)
    step_out = jax.ShapeDtypeStruct((CASES, PAIR), F32)
    terms, step, older = pl.pallas_call(
        kernel,
        out_shape=(terms_out, step_out, step_out),
        in_specs=[hbm] * 6,
        out_specs=(hbm, vmem, vmem),
        scratch_shapes=[
            pltpu.VMEM((3, 2, 4, CASES, PAIR), F32),
            pltpu.VMEM((ROWS, ROWS), jnp.bfloat16),
            pltpu.VMEM((4, PAIR, PAIR), jnp.bfloat16),
            pltpu.VMEM((384, 384), F32),
            pltpu.VMEM((1, 4), jnp.int32),
            pltpu.VMEM((4, PAIR), jnp.int32),
            pltpu.VMEM((528, 512), F32),
            pltpu.VMEM((512, 512), jnp.bfloat16),
            pltpu.VMEM((512, 512), jnp.bfloat16),
            pltpu.VMEM((512, 512), F32),
            pltpu.VMEM((4, 24, PAIR), F32),
            pltpu.VMEM((4, 24, PAIR), F32),
            pltpu.VMEM((4, CASES, PAIR), F32),
            pltpu.VMEM((4, CASES, PAIR), F32),
            pltpu.VMEM((4, CASES, PAIR), F32),
            pltpu.VMEM((4, CASES, PAIR), F32),
            pltpu.VMEM((3, PAIR), F32),
            pltpu.VMEM((NSUB - 1, 8, PAIR), F32),
            pltpu.VMEM((NCL, 8, PAIR), F32),
            pltpu.VMEM((5, PAIR), F32),
            pltpu.VMEM((NSUB - 1, 8, PAIR), F32),
            pltpu.VMEM((NCL, 8, PAIR), F32),
            pltpu.VMEM((1, PAIR), F32),
            pltpu.VMEM((2 * NSUB - 1, PAIR), F32),
            pltpu.VMEM((1, PAIR), F32),
            pltpu.VMEM((CHIPS - 1, PAIR), F32),
            pltpu.SemaphoreType.DMA((13,)),
            pltpu.SemaphoreType.DMA((3, 4)),
            pltpu.SemaphoreType.DMA((3, 4)),
            pltpu.SemaphoreType.DMA((9,)),
            pltpu.SemaphoreType.DMA((9,)),
            pltpu.SemaphoreType.REGULAR((5,)),
        ],
        compiler_params=pltpu.CompilerParams(
            collective_id=0, has_side_effects=True, vmem_limit_bytes=60 * 1024*1024
        ),
        name="feti",
    )(schur, load, jnp.transpose(rigid, (0, 1, 3, 2, 4)), lengths, partner, coarse_inverse)
    return tuple(
        (terms[0, k] + step[None] * terms[1, k] + older[None] * terms[2, k])[None, None] for k in range(2)
    )


def solution(mesh):
    in_specs = (
        P("clus", "sub", None, None),
        P("clus", "sub", None, None, None),
        P("clus", "sub", None, None, None),
        P("clus", "sub", None),
        P("clus", "sub", None, None),
        P(),
    )
    out_specs = (P("clus", "sub", None, None, None), P("clus", "sub", None, None, None))
    return jax.shard_map(shards, mesh=mesh, in_specs=in_specs, out_specs=out_specs, check_vma=False)
```
